512 devices in a mesh: section: 16 (over z), tensor: 32 (over y, x, core).
Axes of the slice: x: 4, y: 4, z: 16, core: 2. Of those that a mesh axis runs over, the one named last changes fastest.
Arguments:
- tokens: bfloat16 [128, 6144], P(None, 'tensor'), may hold values from -6 to 6
- targets: bfloat16 [128, 6144], P(None, 'tensor'), may hold values from -6 to 6
- doc_ids: int32 [128], replicated, may hold values from 0 to 7, never falling along the last dimension, each value on 1 to 32 neighbouring positions
- norm_gains: float32 [16, 6144], P('section'), may hold values from 0.5 to 1.5
- w_qk: bfloat16 [16, 6144, 4096], P('section', None, 'tensor')
- w_val: bfloat16 [16, 6144, 4096], P('section', None, 'tensor'), may hold values from -0.078125 to 0.078125
- w_out: bfloat16 [16, 4096, 6144], P('section', None, 'tensor'), may hold values from -0.09375 to 0.09375
Outputs:
- section_outputs: bfloat16 [16, 128, 6144], P('section', None, 'tensor')
- losses: float32 [8], replicated
The draws below stay inside these ranges and needn't reach their ends.
Inputs may be any that keep to these rules, and one draw needn't show every extreme that they name: `doc_ids`: ids never fall along the row; each of the 8 documents holds 1 to 32 tokens, one exactly 32.
All inputs are finite; a program needn't handle non-finite values.
Results may differ from the reference program's by a relative error of at most 0.03.
Values may be sent and summed in bfloat16 or wider, within the bound.
No kernel may reach another device: no remote copies, remote signals or barrier semaphores. Data moves between devices by JAX's collectives and lax.ppermute only.
A program may use at most 64 MiB of HBM per device.

```python
import math
import jax
import jax.numpy as jnp
import numpy as np
from jax import lax

D = 6144
HD = 64
ROW = 128
DOCS = 8
HEADS = 64
MOST = 32
N_SECTION = 16


def draw_w_qk(key, part):
    key = jax.random.fold_in(key, 11)
    base = jax.random.normal(key, (N_SECTION, D, HEADS * HD), jnp.float32) * D ** (-0.5)
    return base.astype(jnp.bfloat16)


def shard_levels(key, shape, cuts, low, top_value):
    level = 1.0
    for position, shards_of in cuts:
        heights = jax.random.uniform(jax.random.fold_in(jax.random.fold_in(key, 6), position), (shards_of,), jnp.float32, low / len(cuts), top_value / len(cuts))
        level = level * jnp.repeat(jnp.exp(heights), shape[position] // shards_of).reshape((-1,) + (1,) * (len(shape) - 1 - position))
    return level


def profile(amount, total, reach, skew):
    loads = [(1 << 20) // math.isqrt(grade ** skew) + 1 for grade in range(2, amount + 1)]
    spare, counts = total - reach - (amount - 1), [1] * (amount - 1)
    while spare > 0:
        movable = [i for i in range(amount - 1) if counts[i] < reach]
        pool, left = sum([loads[i] for i in movable]), spare
        for i in movable:
            more = min(reach - counts[i], max(1, left * loads[i] // pool), spare)
            counts[i] = counts[i] + more
            spare = spare - more
    return np.array([reach] + counts)


def uneven_parts(stream_key, number_of, total, limit, slope):
    if number_of == 2:
        one = jax.random.randint(stream_key, (), max(1, total - limit), min(limit, total - 1) + 1)
        return jnp.stack([one, total - one])
    sizes = jnp.asarray(profile(number_of, total, limit, slope), jnp.int32)
    couples = (number_of - 1) // 2
    source_of, taker = sizes[1:1 + 2 * couples:2], sizes[2:2 + 2 * couples:2]
    room = jnp.minimum(source_of - 1, limit - taker)
    moved = jax.random.randint(jax.random.fold_in(stream_key, 1), (couples,), 0, 1 << 20) % (room + 1)
    sizes = sizes.at[1:1 + 2 * couples:2].set(source_of - moved).at[2:2 + 2 * couples:2].set(taker + moved)
    return sizes[jax.random.permutation(jax.random.fold_in(stream_key, 2), number_of)]


def normal_values(own_key, dims, scale, bound, cuts=(), held_as=jnp.bfloat16):
    result = jax.random.normal(own_key, dims, jnp.float32) * scale
    if len(cuts) > 0:
        result = shard_levels(own_key, dims, cuts, -0.22, 0.18) * result
    return jnp.clip(result, min=-bound, max=bound).astype(held_as)


def setup_inputs(seed: int = 0) -> dict:
    key_list = jax.random.split(jax.random.key(seed), 8)
    tokens = normal_values(key_list[0], (ROW, D), 1.0, 6.0, ((1, 32),))
    targets = normal_values(key_list[1], (ROW, D), 1.0, 6.0, ((1, 32),))
    doc_ids = jnp.searchsorted(jnp.cumsum(uneven_parts(key_list[2], DOCS, ROW, MOST, 0)), jnp.arange(ROW), side="right").astype(jnp.int32)
    norm_gains = jnp.clip(1.0 + 0.1 * jax.random.normal(key_list[3], (N_SECTION, D), jnp.float32), 0.5, 1.5)
    w_qk = draw_w_qk(jax.random.fold_in(key_list[7], 71), 0)
    w_val = normal_values(key_list[5], (N_SECTION, D, HEADS * HD), D ** -0.5, 0.078125, ((0, 16), (2, 32)))
    w_out = normal_values(key_list[6], (N_SECTION, HEADS * HD, D), (HEADS * HD) ** -0.5, 0.09375, ((0, 16), (2, 32)))
    return dict(tokens=tokens, targets=targets, doc_ids=doc_ids, norm_gains=norm_gains, w_qk=w_qk, w_val=w_val, w_out=w_out)


def reference(tokens, targets, doc_ids, norm_gains, w_qk, w_val, w_out):
    positions = jnp.arange(ROW, dtype=jnp.int32)
    allowed = (positions[None, :] <= positions[:, None]) & (doc_ids[None, :] == doc_ids[:, None])
    hidden = tokens
    results = []
    for layer_num in range(N_SECTION):
        x_float = hidden.astype(jnp.float32)
        row_mean = lax.optimization_barrier(jnp.mean(x_float, -1, keepdims=True))
        centered = x_float - row_mean
        row_var = lax.optimization_barrier(jnp.mean(centered * centered, -1, keepdims=True))
        normed = (centered * lax.rsqrt(row_var + 1e-05) * norm_gains[layer_num][None, :]).astype(jnp.bfloat16)
        qk_rows = jnp.dot(normed, w_qk[layer_num], preferred_element_type=jnp.float32).astype(jnp.bfloat16)
        val_rows = jnp.dot(normed, w_val[layer_num], preferred_element_type=jnp.float32).astype(jnp.bfloat16)
        qk_float = qk_rows.astype(jnp.float32).reshape(ROW, HEADS, HD)
        key_rows = (qk_float * lax.rsqrt(lax.optimization_barrier(jnp.mean(qk_float * qk_float, -1, keepdims=True)) + 1e-06)).astype(jnp.bfloat16)
        scores = jnp.einsum('qhd,khd->hqk', qk_float, key_rows.astype(jnp.float32)) / HD
        masked = jnp.where(allowed[None], scores, -1e+30)
        peak = lax.optimization_barrier(jnp.max(masked, -1, keepdims=True))
        expo = jnp.where(allowed[None], jnp.exp(masked - peak), 0.0)
        weights = (expo / lax.optimization_barrier(jnp.sum(expo, -1, keepdims=True))).astype(jnp.bfloat16)
        val_float = val_rows.astype(jnp.float32).reshape(ROW, HEADS, HD)
        attended = jnp.einsum('hqk,khd->qhd', weights.astype(jnp.float32), val_float).astype(jnp.bfloat16).reshape(ROW, HEADS * HD)
        mixed = jnp.dot(attended, w_out[layer_num], preferred_element_type=jnp.float32)
        hidden = (x_float + mixed).astype(jnp.bfloat16)
        results.append(hidden)
    section_outputs = jnp.stack(results, 0)
    diff = hidden.astype(jnp.float32) - targets.astype(jnp.float32)
    token_sums = lax.optimization_barrier(jnp.sum(diff * diff, -1))
    doc_table = (doc_ids[:, None] == jnp.arange(DOCS, dtype=jnp.int32)[None, :]).astype(jnp.float32)
    doc_sums = lax.optimization_barrier(jnp.sum(doc_table * token_sums[:, None], 0))
    doc_counts = lax.optimization_barrier(jnp.sum(doc_table, 0))
    losses = doc_sums / (doc_counts * D)
    return (section_outputs, losses)
```

```python
import functools

import jax
import jax.numpy as jnp
from jax import lax
from jax.experimental import pallas as pl
from jax.experimental.pallas import tpu as pltpu
from jax.sharding import Mesh
from jax.sharding import PartitionSpec as P

D = 6144
HD = 64
DOCS = 8
MOST = 32
NEG = -1e30
PLANE = ("y", "x")


def qkv_attention(order_ref, rows_ref, gain_ref, w_ref, bias_ref, kin_ref, vin_ref, send_ref, kout_ref, vout_ref):
    chips, length, cols = rows_ref.shape
    width = kin_ref.shape[1]
    heads = width // HD
    total = jnp.zeros((length, cols), jnp.float32)
    for chip in range(chips):
        total += rows_ref[chip].astype(jnp.float32)
    mean = jnp.sum(total, -1, keepdims=True) / (chips * cols)
    total = jnp.zeros((length, cols), jnp.float32)
    for chip in range(chips):
        centered = rows_ref[chip].astype(jnp.float32) - mean
        total += centered * centered
    scale = lax.rsqrt(jnp.sum(total, -1, keepdims=True) / (chips * cols) + 1e-05)
    acc = jnp.zeros((length, 2 * width), jnp.float32)
    for chip in range(chips):
        centered = rows_ref[chip].astype(jnp.float32) - mean
        normed = (centered * scale * gain_ref[chip : chip + 1, :]).astype(jnp.bfloat16)
        acc += jnp.dot(normed, w_ref[chip * cols : (chip + 1) * cols, :], preferred_element_type=jnp.float32)
    rounded = acc.astype(jnp.bfloat16).astype(jnp.float32)
    qk, val = rounded[:, :width], rounded[:, width:]
    head_of = lax.broadcasted_iota(jnp.int32, (length, width), 1) // HD
    squares = qk * qk
    inverse = jnp.zeros((length, width), jnp.float32)
    stack = []
    for head in range(heads):
        mine = head_of == head
        square_mean = jnp.sum(jnp.where(mine, squares, 0.0), -1, keepdims=True) / HD
        inverse = jnp.where(mine, lax.rsqrt(square_mean + 1e-06), inverse)
        stack.append(jnp.where(mine, qk, 0.0))
    key = (qk * inverse).astype(jnp.bfloat16).astype(jnp.float32)
    queries = jnp.concatenate(stack, 0).astype(jnp.bfloat16)
    keys = jnp.concatenate([kin_ref[...], key], 0).astype(jnp.bfloat16)
    vals = jnp.concatenate([vin_ref[...], val], 0).astype(jnp.bfloat16)
    scores = lax.dot_general(queries, keys, (((1,), (1,)), ((), ())), preferred_element_type=jnp.float32) / HD
    scores = scores + bias_ref[order_ref[0]]
    peak = jnp.max(scores, -1, keepdims=True)
    expo = jnp.exp(scores - peak)
    weights = (expo / jnp.sum(expo, -1, keepdims=True)).astype(jnp.bfloat16)
    mixed = jnp.dot(weights, vals, preferred_element_type=jnp.float32)
    attended = jnp.zeros((length, width), jnp.float32)
    for head in range(heads):
        attended = jnp.where(head_of == head, mixed[head * length : (head + 1) * length], attended)
    attended = attended.astype(jnp.bfloat16)
    for chip in range(chips):
        send_ref[chip] = attended
    kout_ref[...] = key
    vout_ref[...] = val


def project_out(heads_ref, w_ref, rows_ref, out_ref):
    chips, _, width = heads_ref.shape
    acc = rows_ref[...].astype(jnp.float32)
    mixed = jnp.zeros(acc.shape, jnp.float32)
    for chip in range(chips):
        mixed += jnp.dot(
            heads_ref[chip], w_ref[chip * width : (chip + 1) * width, :], preferred_element_type=jnp.float32
        )
    out_ref[...] = (acc + mixed).astype(jnp.bfloat16)


def local(tokens, targets, doc_ids, norm_gains, w_qk, w_val, w_out):
    section = lax.axis_index("section")
    section_count = lax.axis_size("section")
    core = lax.axis_index("core")
    chips = lax.axis_size("y") * lax.axis_size("x")
    row_count, cols_own = tokens.shape
    cols = 2 * cols_own
    width = 2 * w_qk.shape[2]
    heads = width // HD
    slices = 2
    length = (row_count // 2 + MOST // 2) // slices
    part = slices * length

    def swap(value):
        return lax.ppermute(value, "core", [(0, 1), (1, 0)])

    def both(own, other):
        return [jnp.where(core == 0, own, other), jnp.where(core == 0, other, own)]

    position = jnp.arange(row_count, dtype=jnp.int32)
    previous = jnp.concatenate([doc_ids[:1] - 1, doc_ids[:-1]])
    far = jnp.abs(position - row_count // 2) * row_count + position
    cut = jnp.min(jnp.where(doc_ids != previous, far, row_count * row_count)) % row_count
    start = jnp.where(core == 0, 0, cut)
    count = jnp.where(core == 0, cut, row_count - cut)
    place = jnp.arange(part, dtype=jnp.int32)
    pick = ((start + place)[:, None] == position[None, :]) & (place < count)[:, None]
    pick_bf = pick.astype(jnp.bfloat16)

    def picked(rows):
        return jnp.dot(pick_bf, rows, preferred_element_type=jnp.float32)

    tokens_chip = jnp.concatenate(both(tokens, swap(tokens)), 1)
    first_rows = picked(tokens_chip).astype(jnp.bfloat16)
    docs = jnp.sum(jnp.where(pick, doc_ids[None, :], 0), 1)
    docs = jnp.where(place < count, docs, DOCS)
    same = (docs[:, None] == docs[None, :]) & (place[None, :] <= place[:, None])
    allowed = jnp.stack(
        [
            jnp.concatenate([jnp.zeros((length, length), bool), same[:length, :length]], 1),
            same[length:],
        ]
    )
    bias = jnp.tile(jnp.where(allowed, 0.0, NEG).astype(jnp.float32), (1, heads, 1))

    w_in = jnp.concatenate(both(w_qk[0], swap(w_qk[0])) + both(w_val[0], swap(w_val[0])), 1)
    w_last = jnp.concatenate(both(w_out[0], swap(w_out[0])), 1)
    gains = norm_gains[0].reshape(chips, cols)

    vmem = pl.BlockSpec(memory_space=pltpu.VMEM)
    smem = pl.BlockSpec(memory_space=pltpu.SMEM)
    params = pltpu.CompilerParams(vmem_limit_bytes=32 * 1024 * 1024)
    attend = pl.pallas_call(
        qkv_attention,
        out_shape=(
            jax.ShapeDtypeStruct((chips, length, width), jnp.bfloat16),
            jax.ShapeDtypeStruct((length, width), jnp.float32),
            jax.ShapeDtypeStruct((length, width), jnp.float32),
        ),
        in_specs=[smem] + [vmem] * 6,
        out_specs=(vmem,) * 3,
        compiler_params=params,
        cost_estimate=pl.CostEstimate(
            flops=2 * length * D * 2 * width, bytes_accessed=4 * D * width, transcendentals=heads * length * part
        ),
    )
    project = pl.pallas_call(
        project_out,
        out_shape=jax.ShapeDtypeStruct((length, cols), jnp.bfloat16),
        in_specs=[vmem] * 3,
        out_specs=vmem,
        compiler_params=params,
        cost_estimate=pl.CostEstimate(
            flops=2 * length * chips * width * cols, bytes_accessed=2 * chips * width * cols, transcendentals=0
        ),
    )

    keys = jnp.zeros((length, width), jnp.float32)
    vals = jnp.zeros((length, width), jnp.float32)
    done = [jnp.zeros((length, cols), jnp.bfloat16) for _ in range(slices)]
    received = jnp.zeros((length, cols), jnp.bfloat16)
    for step in range(section_count + slices - 1):
        order = step - section
        turn = jnp.clip(order, 0, slices - 1)
        mine = min(step, slices - 1)
        rows = jnp.where(section == 0, first_rows[mine * length : (mine + 1) * length], received)
        gathered = lax.all_to_all(
            jnp.broadcast_to(rows[None], (chips,) + rows.shape), PLANE, 0, 0, tiled=True
        )
        send, keys, vals = attend(turn.reshape(1), gathered, gains, w_in, bias, keys, vals)
        attended = lax.all_to_all(send, PLANE, 0, 0, tiled=True)
        rows = project(attended, w_last, rows)
        if step < section_count + slices - 2:
            received = lax.ppermute(rows, "section", [(z, z + 1) for z in range(section_count - 1)])
        done = [jnp.where(order == number, rows, kept) for number, kept in enumerate(done)]

    part_rows = jnp.concatenate(done, 0)
    targets_chip = jnp.concatenate(both(targets, swap(targets)), 1)
    diff = part_rows.astype(jnp.float32) - picked(targets_chip)
    token_sums = jnp.sum(diff * diff, -1)
    doc_names = jnp.arange(128, dtype=jnp.int32)[None, :]
    in_doc = docs[:, None] == doc_names
    sums = jnp.sum(jnp.where(in_doc, token_sums[:, None], 0.0), 0)
    sums = jnp.where((section == section_count - 1) & (doc_names[0] < DOCS), sums, 0.0)

    def share(value, axes):
        number = 1
        for axis in axes:
            number *= lax.axis_size(axis)
        pieces = jnp.broadcast_to(value[None], (number,) + value.shape)
        return jnp.sum(lax.all_to_all(pieces, axes, 0, 0, tiled=True), 0)

    totals = share(share(sums[None], ("y", "x", "core")), ("section",))[0, :DOCS]
    doc_counts = jnp.sum((doc_ids[:, None] == jnp.arange(DOCS, dtype=jnp.int32)[None, :]).astype(jnp.float32), 0)
    losses = totals / (doc_counts * D)

    halves = [part_rows[:, :cols_own], part_rows[:, cols_own:]]
    keep = jnp.where(core == 0, halves[0], halves[1])
    give = jnp.where(core == 0, halves[1], halves[0])
    stacked = jnp.concatenate(both(keep, swap(give)), 0)
    source = jnp.where(position < cut, position, position - cut + part)
    back = (source[:, None] == jnp.arange(2 * part, dtype=jnp.int32)[None, :]).astype(jnp.bfloat16)
    section_rows = jnp.dot(back, stacked, preferred_element_type=jnp.float32).astype(jnp.bfloat16)
    return (section_rows[None], losses)


def solution(mesh):
    names = ("section", "y", "x", "core")
    fine = Mesh(mesh.devices.reshape(mesh.devices.shape[0], 4, 4, 2), names)
    tensor = ("y", "x", "core")
    placed = (
        P(None, tensor),
        P(None, tensor),
        P(),
        P("section", None),
        P("section", None, tensor),
        P("section", None, tensor),
        P("section", None, tensor),
    )
    return jax.shard_map(
        local,
        mesh=fine,
        in_specs=placed,
        out_specs=(P("section", None, tensor), P()),
        check_vma=False,
    )
```

```python
import jax
import jax.numpy as jnp
from jax import lax
from jax.experimental import pallas as pl
from jax.experimental.pallas import tpu as pltpu
from jax.sharding import Mesh
from jax.sharding import PartitionSpec as P

D = 6144
HD = 64
DOCS = 8
MOST = 32
NEG = -1e30
PLANE = ("y", "x")


def qkv_attention(
    flag_ref, rows_ref, gain_ref, w_ref, bias_ref, kin_ref, vin_ref, send_ref, kout_ref, vout_ref, next_ref
):
    chips, length, cols = rows_ref.shape
    width = kin_ref.shape[1]
    heads = width // HD
    total = jnp.zeros((length, cols), jnp.float32)
    for chip in range(chips):
        total += rows_ref[chip].astype(jnp.float32)
    mean = jnp.sum(total, -1, keepdims=True) / (chips * cols)
    total = jnp.zeros((length, cols), jnp.float32)
    for chip in range(chips):
        centered = rows_ref[chip].astype(jnp.float32) - mean
        total += centered * centered
    scale = lax.rsqrt(jnp.sum(total, -1, keepdims=True) / (chips * cols) + 1e-05)
    acc = jnp.zeros((length, 2 * width), jnp.float32)
    for chip in range(chips):
        centered = rows_ref[chip].astype(jnp.float32) - mean
        normed = (centered * scale * gain_ref[chip : chip + 1, :]).astype(jnp.bfloat16)
        acc += jnp.dot(normed, w_ref[chip * cols : (chip + 1) * cols, :], preferred_element_type=jnp.float32)
    rounded = acc.astype(jnp.bfloat16).astype(jnp.float32)
    qk, val = rounded[:, :width], rounded[:, width:]
    head_of = lax.broadcasted_iota(jnp.int32, (length, width), 1) // HD
    squares = qk * qk
    inverse = jnp.zeros((length, width), jnp.float32)
    stack = []
    for head in range(heads):
        mine = head_of == head
        square_mean = jnp.sum(jnp.where(mine, squares, 0.0), -1, keepdims=True) / HD
        inverse = jnp.where(mine, lax.rsqrt(square_mean + 1e-06), inverse)
        stack.append(jnp.where(mine, qk, 0.0))
    key = (qk * inverse).astype(jnp.bfloat16).astype(jnp.float32)
    queries = jnp.concatenate(stack, 0).astype(jnp.bfloat16)
    keys = jnp.concatenate([kin_ref[...], key], 0).astype(jnp.bfloat16)
    vals = jnp.concatenate([vin_ref[...], val], 0).astype(jnp.bfloat16)
    scores = lax.dot_general(queries, keys, (((1,), (1,)), ((), ())), preferred_element_type=jnp.float32) / HD
    scores = scores + jnp.where(flag_ref[0:1, 0:1] > 0.0, bias_ref[1], bias_ref[0])
    peak = jnp.max(scores, -1, keepdims=True)
    expo = jnp.exp(scores - peak)
    weights = (expo / jnp.sum(expo, -1, keepdims=True)).astype(jnp.bfloat16)
    mixed = jnp.dot(weights, vals, preferred_element_type=jnp.float32)
    attended = jnp.zeros((length, width), jnp.float32)
    for head in range(heads):
        attended = jnp.where(head_of == head, mixed[head * length : (head + 1) * length], attended)
    attended = attended.astype(jnp.bfloat16)
    for chip in range(chips):
        send_ref[chip] = attended
    kout_ref[...] = key
    vout_ref[...] = val
    is_order = lax.broadcasted_iota(jnp.int32, flag_ref.shape, 0) == 0
    next_ref[...] = flag_ref[...] + jnp.where(is_order, 1.0, 0.0)


def project_out(flag_ref, heads_ref, w_ref, rows_ref, kept_ref, out_ref, done_ref):
    chips, _, width = heads_ref.shape
    acc = rows_ref[...].astype(jnp.float32)
    mixed = jnp.zeros(acc.shape, jnp.float32)
    for chip in range(chips):
        mixed += jnp.dot(
            heads_ref[chip], w_ref[chip * width : (chip + 1) * width, :], preferred_element_type=jnp.float32
        )
    rows = (acc + mixed).astype(jnp.bfloat16)
    out_ref[...] = rows
    for number in range(kept_ref.shape[0]):
        mine = flag_ref[0:1, 0:1] == float(number)
        done_ref[number] = jnp.where(mine, rows.astype(jnp.float32), kept_ref[number].astype(jnp.float32)).astype(
            jnp.bfloat16
        )


def spread(flag_ref, tokens_ref, received_ref, rows_ref, send_ref):
    first = flag_ref[1:2, 0:1] > 0.0
    rows = jnp.where(first, tokens_ref[...].astype(jnp.float32), received_ref[...].astype(jnp.float32))
    rows = rows.astype(jnp.bfloat16)
    rows_ref[...] = rows
    for chip in range(send_ref.shape[0]):
        send_ref[chip] = rows


def local(tokens, targets, doc_ids, norm_gains, w_qk, w_val, w_out):
    section = lax.axis_index("section")
    section_count = lax.axis_size("section")
    core = lax.axis_index("core")
    chips = lax.axis_size("y") * lax.axis_size("x")
    row_count, cols_own = tokens.shape
    cols = 2 * cols_own
    width = 2 * w_qk.shape[2]
    heads = width // HD
    slices = 2
    length = (row_count // 2 + MOST // 2) // slices
    part = slices * length

    def swap(value):
        return lax.ppermute(value, "core", [(0, 1), (1, 0)])

    def both(own, other):
        return [jnp.where(core == 0, own, other), jnp.where(core == 0, other, own)]

    position = jnp.arange(row_count, dtype=jnp.int32)
    previous = jnp.concatenate([doc_ids[:1] - 1, doc_ids[:-1]])
    far = jnp.abs(position - row_count // 2) * row_count + position
    cut = jnp.min(jnp.where(doc_ids != previous, far, row_count * row_count)) % row_count
    start = jnp.where(core == 0, 0, cut)
    count = jnp.where(core == 0, cut, row_count - cut)
    place = jnp.arange(part, dtype=jnp.int32)
    pick = ((start + place)[:, None] == position[None, :]) & (place < count)[:, None]
    pick_bf = pick.astype(jnp.bfloat16)

    def picked(rows):
        return jnp.dot(pick_bf, rows, preferred_element_type=jnp.float32)

    tokens_chip = jnp.concatenate(both(tokens, swap(tokens)), 1)
    first_rows = picked(tokens_chip).astype(jnp.bfloat16)
    first_parts = [first_rows[number * length : (number + 1) * length] for number in range(slices)]
    docs = jnp.sum(jnp.where(pick, doc_ids[None, :], 0), 1)
    docs = jnp.where(place < count, docs, DOCS)
    same = (docs[:, None] == docs[None, :]) & (place[None, :] <= place[:, None])
    allowed = jnp.stack(
        [
            jnp.concatenate([jnp.zeros((length, length), bool), same[:length, :length]], 1),
            same[length:],
        ]
    )
    bias = jnp.tile(jnp.where(allowed, 0.0, NEG).astype(jnp.float32), (1, heads, 1))

    w_in = jnp.concatenate(both(w_qk[0], swap(w_qk[0])) + both(w_val[0], swap(w_val[0])), 1)
    w_out_t = jnp.swapaxes(w_out[0], 0, 1)
    w_last = jnp.swapaxes(jnp.concatenate(both(w_out_t, swap(w_out_t)), 0), 0, 1)
    gains = norm_gains[0].reshape(chips, cols)

    vmem = pl.BlockSpec(memory_space=pltpu.VMEM)
    params = pltpu.CompilerParams(vmem_limit_bytes=16 * 1024 * 1024)
    flag_tile = jax.ShapeDtypeStruct((8, 128), jnp.float32)
    attend = pl.pallas_call(
        qkv_attention,
        out_shape=(
            jax.ShapeDtypeStruct((chips, length, width), jnp.bfloat16),
            jax.ShapeDtypeStruct((length, width), jnp.float32),
            jax.ShapeDtypeStruct((length, width), jnp.float32),
            flag_tile,
        ),
        in_specs=[vmem] * 7,
        out_specs=(vmem,) * 4,
        compiler_params=params,
        cost_estimate=pl.CostEstimate(
            flops=2 * length * D * 2 * width, bytes_accessed=4 * D * width, transcendentals=heads * length * part
        ),
    )
    project = pl.pallas_call(
        project_out,
        out_shape=(
            jax.ShapeDtypeStruct((length, cols), jnp.bfloat16),
            jax.ShapeDtypeStruct((slices, length, cols), jnp.bfloat16),
        ),
        in_specs=[vmem] * 5,
        out_specs=(vmem,) * 2,
        compiler_params=params,
        cost_estimate=pl.CostEstimate(
            flops=2 * length * chips * width * cols, bytes_accessed=2 * chips * width * cols, transcendentals=0
        ),
    )

    place_rows = pl.pallas_call(
        spread,
        out_shape=(
            jax.ShapeDtypeStruct((length, cols), jnp.bfloat16),
            jax.ShapeDtypeStruct((chips, length, cols), jnp.bfloat16),
        ),
        in_specs=[vmem] * 3,
        out_specs=(vmem,) * 2,
        compiler_params=params,
        cost_estimate=pl.CostEstimate(flops=0, bytes_accessed=2 * chips * length * cols, transcendentals=0),
    )
    tile_row = lax.broadcasted_iota(jnp.int32, flag_tile.shape, 0)
    flags = jnp.where(
        tile_row == 0, -section.astype(jnp.float32), jnp.where((tile_row == 1) & (section == 0), 1.0, 0.0)
    )
    targets_chip = jnp.concatenate(both(targets, swap(targets)), 1)
    goal = picked(targets_chip)

    keys = jnp.zeros((length, width), jnp.float32)
    vals = jnp.zeros((length, width), jnp.float32)
    done = jnp.zeros((slices, length, cols), jnp.bfloat16)
    received = jnp.zeros((length, cols), jnp.bfloat16)
    for step in range(section_count + slices - 1):
        mine = min(step, slices - 1)
        rows, send = place_rows(flags, first_parts[mine], received)
        gathered = lax.all_to_all(send, PLANE, 0, 0, tiled=True)
        send, keys, vals, next_flags = attend(flags, gathered, gains, w_in, bias, keys, vals)
        attended = lax.all_to_all(send, PLANE, 0, 0, tiled=True)
        if step == 0:
            attended, goal, w_last, first_parts = lax.optimization_barrier((attended, goal, w_last, first_parts))
        rows, done = project(flags, attended, w_last, rows, done)
        flags = next_flags
        if step < section_count + slices - 2:
            received = lax.ppermute(rows, "section", [(z, z + 1) for z in range(section_count - 1)])

    part_rows = done.reshape(part, cols)
    diff = part_rows.astype(jnp.float32) - goal
    token_sums = jnp.sum(diff * diff, -1)
    doc_names = jnp.arange(128, dtype=jnp.int32)[None, :]
    in_doc = docs[:, None] == doc_names
    sums = jnp.sum(jnp.where(in_doc, token_sums[:, None], 0.0), 0)
    sums = jnp.where((section == section_count - 1) & (doc_names[0] < DOCS), sums, 0.0)

    def share(value, axes):
        number = 1
        for axis in axes:
            number *= lax.axis_size(axis)
        pieces = jnp.broadcast_to(value[None], (number,) + value.shape)
        return jnp.sum(lax.all_to_all(pieces, axes, 0, 0, tiled=True), 0)

    totals = share(share(sums[None], ("y", "x", "core")), ("section",))[0, :DOCS]
    doc_counts = jnp.sum((doc_ids[:, None] == jnp.arange(DOCS, dtype=jnp.int32)[None, :]).astype(jnp.float32), 0)
    losses = totals / (doc_counts * D)

    halves = [part_rows[:, :cols_own], part_rows[:, cols_own:]]
    keep = jnp.where(core == 0, halves[0], halves[1])
    give = jnp.where(core == 0, halves[1], halves[0])
    stacked = jnp.concatenate(both(keep, swap(give)), 0)
    source = jnp.where(position < cut, position, position - cut + part)
    back = (source[:, None] == jnp.arange(2 * part, dtype=jnp.int32)[None, :]).astype(jnp.bfloat16)
    section_rows = jnp.dot(back, stacked, preferred_element_type=jnp.float32).astype(jnp.bfloat16)
    return (section_rows[None], losses)


def solution(mesh):
    names = ("section", "y", "x", "core")
    fine = Mesh(mesh.devices.reshape(mesh.devices.shape[0], 4, 4, 2), names)
    tensor = ("y", "x", "core")
    placed = (
        P(None, tensor),
        P(None, tensor),
        P(),
        P("section", None),
        P("section", None, tensor),
        P("section", None, tensor),
        P("section", None, tensor),
    )
    return jax.shard_map(
        local,
        mesh=fine,
        in_specs=placed,
        out_specs=(P("section", None, tensor), P()),
        check_vma=False,
    )
```

```python
import jax
import jax.numpy as jnp
from jax import lax
from jax.experimental import pallas as pl
from jax.experimental.pallas import tpu as pltpu
from jax.sharding import Mesh
from jax.sharding import PartitionSpec as P

D = 6144
HD = 64
DOCS = 8
MOST = 32
NEG = -1e30
PLANE = ("y", "x")
BF = jnp.bfloat16
F32 = jnp.float32


def iota(shape, axis):
    return lax.broadcasted_iota(jnp.int32, shape, axis)


def in_core_order(own, other):
    first = lax.axis_index("core") == 0
    return jnp.concatenate([jnp.where(first, own, other), jnp.where(first, other, own)], -1)


def dot(a, b, contract=((1,), (0,))):
    return lax.dot_general(a, b, (contract, ((), ())), preferred_element_type=F32)


def prepare(doc_ref, own_ref, other_ref, pick_ref, bias_ref, rows_ref, flag_ref):
    _, part, count = pick_ref.shape
    length = rows_ref.shape[1]
    doc_j = jnp.broadcast_to(doc_ref[...].astype(F32), (count, count))
    same = jnp.where(doc_j == jnp.transpose(doc_j), 1.0, 0.0)
    before = jnp.where(iota((count, count), 0) < iota((count, count), 1), same, 0.0)
    starts = jnp.sum(before, 0, keepdims=True) == 0.0
    lane = iota((1, count), 1)
    far = (jnp.abs(lane - count // 2) * count + lane).astype(F32)
    nearest = jnp.min(jnp.where(starts, far, float(count * count)), -1, keepdims=True)
    cut = nearest - count * jnp.floor(nearest / count)
    token = iota((part, count), 1).astype(F32)
    slot = iota((part, count), 0).astype(F32)
    picks = [
        jnp.where((token == slot) & (slot < cut), 1.0, 0.0),
        jnp.where(token == slot + cut, 1.0, 0.0),
    ]
    for core in range(2):
        pick_ref[core] = picks[core].astype(BF)
    pick = jnp.where(lax.axis_index("core") == 0, picks[0], picks[1])
    pick_bf = pick.astype(BF)
    rows = in_core_order(dot(pick_bf, own_ref[...]), dot(pick_bf, other_ref[...])).astype(F32)
    for number in range(part // length):
        rows_ref[number] = rows[number * length : (number + 1) * length].astype(BF)
    shifted = jnp.concatenate([jnp.zeros((length, count), F32), pick[: part - length]], 0)
    same_bf = same.astype(BF)
    for number, (queries, keys) in enumerate(((pick[:length], shifted), (pick[length:], pick))):
        alike = dot(dot(queries.astype(BF), same_bf).astype(BF), keys.astype(BF), ((1,), (1,)))
        query_at = iota((length, part), 0) + length
        key_at = iota((length, part), 1)
        allowed = ((alike > 0.5) & (key_at <= query_at)) | (key_at == query_at)
        bias_ref[number] = jnp.where(allowed, 0.0, NEG)
    section = lax.axis_index("section")
    row = iota(flag_ref.shape, 0)
    order = jnp.where(row == 0, -section, 0)
    flag_ref[...] = jnp.where((row == 1) & (section == 0), 1, order).astype(F32)


def qkv_attention(
    flag_ref,
    rows_ref,
    gain_ref,
    w_ref,
    bias_ref,
    kin_ref,
    vin_ref,
    send_ref,
    kout_ref,
    vout_ref,
    next_ref,
):
    chips, length, cols = rows_ref.shape
    width = kin_ref.shape[1]
    heads = width // HD
    total = jnp.zeros((length, cols), F32)
    for chip in range(chips):
        total += rows_ref[chip].astype(F32)
    mean = jnp.sum(total, -1, keepdims=True) / (chips * cols)
    total = jnp.zeros((length, cols), F32)
    for chip in range(chips):
        centered = rows_ref[chip].astype(F32) - mean
        total += centered * centered
    scale = lax.rsqrt(jnp.sum(total, -1, keepdims=True) / (chips * cols) + 1e-05)
    acc = jnp.zeros((length, 2 * width), F32)
    for chip in range(chips):
        span = slice(chip * cols, (chip + 1) * cols)
        centered = rows_ref[chip].astype(F32) - mean
        normed = (centered * scale * gain_ref[:, span]).astype(BF)
        acc += dot(normed, w_ref[span, :])
    rounded = acc.astype(BF).astype(F32)
    qk, val = rounded[:, :width], rounded[:, width:]
    head_of = iota((length, width), 1) // HD
    squares = qk * qk
    inverse = jnp.zeros((length, width), F32)
    stack = []
    for head in range(heads):
        mine = head_of == head
        square_mean = jnp.sum(jnp.where(mine, squares, 0.0), -1, keepdims=True) / HD
        inverse = jnp.where(mine, lax.rsqrt(square_mean + 1e-06), inverse)
        stack.append(jnp.where(mine, qk, 0.0))
    key = (qk * inverse).astype(BF).astype(F32)
    queries = jnp.concatenate(stack, 0).astype(BF)
    keys = jnp.concatenate([kin_ref[...], key], 0).astype(BF)
    vals = jnp.concatenate([vin_ref[...], val], 0).astype(BF)
    bias = jnp.where(flag_ref[0:1, 0:1] > 0.0, bias_ref[1], bias_ref[0])
    scores = dot(queries, keys, ((1,), (1,))) / HD + jnp.concatenate([bias] * heads, 0)
    peak = jnp.max(scores, -1, keepdims=True)
    expo = jnp.exp(scores - peak)
    weights = (expo / jnp.sum(expo, -1, keepdims=True)).astype(BF)
    mixed = dot(weights, vals)
    attended = jnp.zeros((length, width), F32)
    for head in range(heads):
        attended = jnp.where(head_of == head, mixed[head * length : (head + 1) * length], attended)
    half = width // 2
    attended = in_core_order(attended[:, :half], attended[:, half:]).astype(BF)
    for chip in range(chips):
        send_ref[chip] = attended
    kout_ref[...] = key
    vout_ref[...] = val
    next_ref[...] = flag_ref[...] + jnp.where(iota(flag_ref.shape, 0) == 0, 1.0, 0.0)


def pack(*refs):
    *parts, out_ref = refs
    begin = 0
    for ref in parts:
        out_ref[:, begin : begin + ref.shape[1]] = ref[...]
        begin += ref.shape[1]


def project_out(flag_ref, heads_ref, w_ref, rows_ref, kept_ref, out_ref, done_ref):
    chips, _, width = heads_ref.shape
    mixed = jnp.zeros(rows_ref.shape, F32)
    for chip in range(chips):
        mixed += dot(heads_ref[chip], w_ref[chip * width : (chip + 1) * width, :])
    rows = (rows_ref[...].astype(F32) + mixed).astype(BF)
    out_ref[...] = rows
    for number in range(kept_ref.shape[0]):
        mine = flag_ref[0:1, 0:1] == float(number)
        done_ref[number] = jnp.where(mine, rows.astype(F32), kept_ref[number].astype(F32)).astype(BF)


def spread(flag_ref, tokens_ref, received_ref, rows_ref, send_ref):
    first = flag_ref[1:2, 0:1] > 0.0
    rows = jnp.where(first, tokens_ref[...].astype(F32), received_ref[...].astype(F32)).astype(BF)
    rows_ref[...] = rows
    for chip in range(send_ref.shape[0]):
        send_ref[chip] = rows


def aim(pick_ref, own_ref, other_ref, goal_ref):
    pick = pick_ref[lax.axis_index("core")]
    goal_ref[...] = in_core_order(dot(pick, own_ref[...]), dot(pick, other_ref[...]))


def token_errors(pick_ref, done_ref, goal_ref, send_ref):
    slices, length, cols = done_ref.shape
    pick = pick_ref[lax.axis_index("core")].astype(F32)
    total = jnp.zeros((1, pick.shape[1]), F32)
    for number in range(slices):
        span = slice(number * length, (number + 1) * length)
        diff = done_ref[number].astype(F32) - goal_ref[span, :]
        sums = jnp.sum(diff * diff, -1, keepdims=True)
        total += jnp.sum(jnp.where(pick[span] > 0.0, sums, 0.0), 0, keepdims=True)
    last = lax.axis_index("section") == lax.axis_size("section") - 1
    total = jnp.where(last, total, 0.0)
    for number in range(send_ref.shape[0]):
        send_ref[number] = total


def add_up(pieces_ref, send_ref):
    total = pieces_ref[0]
    for number in range(1, pieces_ref.shape[0]):
        total += pieces_ref[number]
    for number in range(send_ref.shape[0]):
        send_ref[number] = total


def finish_losses(pieces_ref, doc_ref, loss_ref):
    total = pieces_ref[0]
    for number in range(1, pieces_ref.shape[0]):
        total += pieces_ref[number]
    count = doc_ref.shape[1]
    mine = doc_ref[...] == iota((DOCS, count), 0)
    sums = jnp.sum(jnp.where(mine, total, 0.0), -1, keepdims=True)
    tokens = jnp.sum(jnp.where(mine, 1.0, 0.0), -1, keepdims=True)
    loss_ref[...] = jnp.broadcast_to(sums / (tokens * D), (DOCS, count))


def place_back(pick_ref, parts_ref, out_ref):
    out_ref[...] = (
        dot(pick_ref[0], parts_ref[0], ((0,), (0,))) + dot(pick_ref[1], parts_ref[1], ((0,), (0,)))
    ).astype(BF)


VMEM = pl.BlockSpec(memory_space=pltpu.VMEM)


def run(kernel, outs, *args, flops=0, bytes_accessed=1 << 16):
    several = isinstance(outs, list)
    shapes = [jax.ShapeDtypeStruct(shape, kind) for shape, kind in (outs if several else [outs])]
    return pl.pallas_call(
        kernel,
        out_shape=shapes if several else shapes[0],
        in_specs=[VMEM] * len(args),
        out_specs=[VMEM] * len(shapes) if several else VMEM,
        compiler_params=pltpu.CompilerParams(vmem_limit_bytes=24 * 1024 * 1024),
        cost_estimate=pl.CostEstimate(flops=flops, bytes_accessed=bytes_accessed, transcendentals=0),
    )(*args)


def local(tokens, targets, doc_ids, norm_gains, w_qk, w_val, w_out):
    core = lax.axis_index("core")
    sections = lax.axis_size("section")
    chips = lax.axis_size("y") * lax.axis_size("x")
    row_count, cols_own = tokens.shape
    cols = 2 * cols_own
    width = 2 * w_qk.shape[2]
    slices = 2
    length = (row_count // 2 + MOST // 2) // slices
    part = slices * length

    def swap(value):
        return lax.ppermute(value, "core", [(0, 1), (1, 0)])

    docs = doc_ids.reshape(1, row_count)
    picks, bias, first_parts, flags = run(
        prepare,
        [
            ((2, part, row_count), BF),
            ((slices, length, part), F32),
            ((slices, length, cols), BF),
            ((8, 128), F32),
        ],
        docs,
        tokens,
        swap(tokens),
    )

    keys = jnp.zeros((length, width), F32)
    vals = jnp.zeros((length, width), F32)
    done = jnp.zeros((slices, length, cols), BF)
    received = jnp.zeros((length, cols), BF)
    goal = w_last = w_in = None
    for step in range(sections + slices - 1):
        rows, send = run(
            spread,
            [((length, cols), BF), ((chips, length, cols), BF)],
            flags,
            first_parts[min(step, slices - 1)],
            received,
        )
        if step == 0:
            w_qk, w_val, w_out, targets, send = lax.optimization_barrier((w_qk, w_val, w_out, targets, send))
            w_in = run(pack, ((D, 2 * width), BF), w_qk[0], swap(w_qk[0]), w_val[0], swap(w_val[0]))
            w_out_t = jnp.swapaxes(w_out[0], 0, 1)
            w_out_other = swap(w_out_t)
            targets_other = swap(targets)
        gathered = lax.all_to_all(send, PLANE, 0, 0, tiled=True)
        send, keys, vals, next_flags = run(
            qkv_attention,
            [((chips, length, width), BF), ((length, width), F32), ((length, width), F32), ((8, 128), F32)],
            flags,
            gathered,
            norm_gains,
            w_in,
            bias,
            keys,
            vals,
            flops=4 * length * D * width,
            bytes_accessed=4 * D * width,
        )
        if step == 0:
            w_out_t, send = lax.optimization_barrier((w_out_t, send))
            w_last = jnp.concatenate(
                [jnp.where(core == 0, w_out_t, w_out_other), jnp.where(core == 0, w_out_other, w_out_t)], 0
            )
            w_last = jnp.swapaxes(w_last, 0, 1)
            goal = run(aim, ((part, cols), F32), picks, targets, targets_other)
        attended = lax.all_to_all(send, PLANE, 0, 0, tiled=True)
        if step == 0:
            attended, goal, w_last, first_parts = lax.optimization_barrier((attended, goal, w_last, first_parts))
        rows, done = run(
            project_out,
            [((length, cols), BF), ((slices, length, cols), BF)],
            flags,
            attended,
            w_last,
            rows,
            done,
            flops=2 * length * chips * width * cols,
            bytes_accessed=2 * chips * width * cols,
        )
        flags = next_flags
        hops = [(z, z + 1) for z in range(sections - 1) if 0 <= step - z < slices]
        if hops:
            received = lax.ppermute(rows, "section", hops)

    send = run(token_errors, ((2 * chips, 1, row_count), F32), picks, done, goal)
    send = lax.all_to_all(send, PLANE + ("core",), 0, 0, tiled=True)
    send = run(add_up, ((sections, 1, row_count), F32), send)
    send = lax.all_to_all(send, "section", 0, 0, tiled=True)
    losses = run(finish_losses, ((DOCS, row_count), F32), send, docs)[:, 0]

    part_rows = done.reshape(part, cols)
    halves = [part_rows[:, :cols_own], part_rows[:, cols_own:]]
    keep = jnp.where(core == 0, halves[0], halves[1])
    other = swap(jnp.where(core == 0, halves[1], halves[0]))
    parts = jnp.stack([jnp.where(core == 0, keep, other), jnp.where(core == 0, other, keep)])
    section_rows = run(place_back, ((row_count, cols_own), BF), picks, parts)
    return (section_rows[None], losses)


def solution(mesh):
    names = ("section", "y", "x", "core")
    fine = Mesh(mesh.devices.reshape(mesh.devices.shape[0], 4, 4, 2), names)
    tensor = ("y", "x", "core")
    placed = (
        P(None, tensor),
        P(None, tensor),
        P(),
        P("section", None),
        P("section", None, tensor),
        P("section", None, tensor),
        P("section", None, tensor),
    )
    return jax.shard_map(
        local,
        mesh=fine,
        in_specs=placed,
        out_specs=(P("section", None, tensor), P()),
        check_vma=False,
    )
```

```python
import jax
import jax.numpy as jnp
from jax import lax
from jax.experimental import pallas as pl
from jax.experimental.pallas import tpu as pltpu
from jax.sharding import Mesh
from jax.sharding import PartitionSpec as P

D = 6144
HD = 64
DOCS = 8
MOST = 32
NEG = -1e30
PLANE = ("y", "x")
BF = jnp.bfloat16
F32 = jnp.float32


def iota(shape, axis):
    return lax.broadcasted_iota(jnp.int32, shape, axis)


def in_core_order(own, other):
    first = lax.axis_index("core") == 0
    return jnp.concatenate([jnp.where(first, own, other), jnp.where(first, other, own)], -1)


def dot(a, b, contract=((1,), (0,))):
    return lax.dot_general(a, b, (contract, ((), ())), preferred_element_type=F32)


def prepare(doc_ref, own_ref, other_ref, pick_ref, bias_ref, rows_ref, flag_ref):
    _, part, count = pick_ref.shape
    length = rows_ref.shape[1]
    doc_j = jnp.broadcast_to(doc_ref[...].astype(F32), (count, count))
    same = jnp.where(doc_j == jnp.transpose(doc_j), 1.0, 0.0)
    before = jnp.where(iota((count, count), 0) < iota((count, count), 1), same, 0.0)
    starts = jnp.sum(before, 0, keepdims=True) == 0.0
    lane = iota((1, count), 1)
    far = (jnp.abs(lane - count // 2) * count + lane).astype(F32)
    nearest = jnp.min(jnp.where(starts, far, float(count * count)), -1, keepdims=True)
    cut = nearest - count * jnp.floor(nearest / count)
    token = iota((part, count), 1).astype(F32)
    slot = iota((part, count), 0).astype(F32)
    picks = [
        jnp.where((token == slot) & (slot < cut), 1.0, 0.0),
        jnp.where(token == slot + cut, 1.0, 0.0),
    ]
    for core in range(2):
        pick_ref[core] = picks[core].astype(BF)
    pick = jnp.where(lax.axis_index("core") == 0, picks[0], picks[1])
    pick_bf = pick.astype(BF)
    rows = in_core_order(*[dot(pick_bf, ref[...], ((1,), (1,))) for ref in (own_ref, other_ref)])
    for number in range(part // length):
        rows_ref[number] = rows[number * length : (number + 1) * length].astype(BF)
    shifted = jnp.concatenate([jnp.zeros((length, count), F32), pick[: part - length]], 0)
    same_bf = same.astype(BF)
    for number, (queries, keys) in enumerate(((pick[:length], shifted), (pick[length:], pick))):
        alike = dot(dot(queries.astype(BF), same_bf).astype(BF), keys.astype(BF), ((1,), (1,)))
        query_at = iota((length, part), 0) + length
        key_at = iota((length, part), 1)
        allowed = ((alike > 0.5) & (key_at <= query_at)) | (key_at == query_at)
        bias_ref[number] = jnp.where(allowed, 0.0, NEG)
    section = lax.axis_index("section")
    row = iota(flag_ref.shape, 0)
    order = jnp.where(row == 0, -section, 0)
    flag_ref[...] = jnp.where((row == 1) & (section == 0), 1, order).astype(F32)


def qkv_attention(
    flag_ref,
    rows_ref,
    gain_ref,
    w_ref,
    bias_ref,
    kin_ref,
    vin_ref,
    send_ref,
    kout_ref,
    vout_ref,
    next_ref,
):
    chips, length, cols = rows_ref.shape
    width = kin_ref.shape[1]
    heads = width // HD
    total = jnp.zeros((length, cols), F32)
    for chip in range(chips):
        total += rows_ref[chip].astype(F32)
    mean = jnp.sum(total, -1, keepdims=True) / (chips * cols)
    total = jnp.zeros((length, cols), F32)
    for chip in range(chips):
        centered = rows_ref[chip].astype(F32) - mean
        total += centered * centered
    scale = lax.rsqrt(jnp.sum(total, -1, keepdims=True) / (chips * cols) + 1e-05)
    acc = jnp.zeros((length, 2 * width), F32)
    for chip in range(chips):
        span = slice(chip * cols, (chip + 1) * cols)
        centered = rows_ref[chip].astype(F32) - mean
        normed = (centered * scale * gain_ref[:, span]).astype(BF)
        acc += dot(normed, w_ref[span, :])
    rounded = acc.astype(BF).astype(F32)
    qk, val = rounded[:, :width], rounded[:, width:]
    head_of = iota((length, width), 1) // HD
    squares = qk * qk
    inverse = jnp.zeros((length, width), F32)
    stack = []
    for head in range(heads):
        mine = head_of == head
        square_mean = jnp.sum(jnp.where(mine, squares, 0.0), -1, keepdims=True) / HD
        inverse = jnp.where(mine, lax.rsqrt(square_mean + 1e-06), inverse)
        stack.append(jnp.where(mine, qk, 0.0))
    key = (qk * inverse).astype(BF).astype(F32)
    queries = jnp.concatenate(stack, 0).astype(BF)
    keys = jnp.concatenate([kin_ref[...], key], 0).astype(BF)
    vals = jnp.concatenate([vin_ref[...], val], 0).astype(BF)
    bias = jnp.where(flag_ref[0:1, 0:1] > 0.0, bias_ref[1], bias_ref[0])
    scores = dot(queries, keys, ((1,), (1,))) / HD + jnp.concatenate([bias] * heads, 0)
    peak = jnp.max(scores, -1, keepdims=True)
    expo = jnp.exp(scores - peak)
    weights = (expo / jnp.sum(expo, -1, keepdims=True)).astype(BF)
    mixed = dot(weights, vals)
    attended = jnp.zeros((length, width), F32)
    for head in range(heads):
        attended = jnp.where(head_of == head, mixed[head * length : (head + 1) * length], attended)
    half = width // 2
    attended = in_core_order(attended[:, :half], attended[:, half:]).astype(BF)
    for chip in range(chips):
        send_ref[chip] = attended
    kout_ref[...] = key
    vout_ref[...] = val
    next_ref[...] = flag_ref[...] + jnp.where(iota(flag_ref.shape, 0) == 0, 1.0, 0.0)


def stage(qk_ref, qk_other_ref, val_ref, val_other_ref, out_ref, out_other_ref, in_ref, last_ref, *scratch):
    own, other, packed, turned, sems = scratch
    width = qk_ref.shape[1]
    copies = [(out_ref, own), (out_other_ref, other)]
    for number, ref in enumerate((qk_ref, qk_other_ref, val_ref, val_other_ref)):
        copies.append((ref, packed.at[:, pl.ds(number * width, width)]))
    copies += [(packed, in_ref), (turned, last_ref)]
    copies = [pltpu.make_async_copy(*pair, sems.at[number]) for number, pair in enumerate(copies)]
    for copy in copies[:6]:
        copy.start()
    for copy in copies[:6]:
        copy.wait()
    copies[6].start()
    block = 256
    first = lax.axis_index("core") == 0
    for begin in range(0, own.shape[1], block):
        span = slice(begin, begin + block)
        here, there = own[:, span], other[:, span]
        here, there = jnp.where(first, here, there), jnp.where(first, there, here)
        turned[span, :] = jnp.transpose(jnp.concatenate([here, there], 0))
    copies[7].start()
    copies[6].wait()
    copies[7].wait()


def project_out(flag_ref, heads_ref, w_ref, rows_ref, kept_ref, out_ref, done_ref):
    chips, _, width = heads_ref.shape
    mixed = jnp.zeros(rows_ref.shape, F32)
    for chip in range(chips):
        mixed += dot(heads_ref[chip], w_ref[chip * width : (chip + 1) * width, :])
    rows = (rows_ref[...].astype(F32) + mixed).astype(BF)
    out_ref[...] = rows
    for number in range(kept_ref.shape[0]):
        mine = flag_ref[0:1, 0:1] == float(number)
        done_ref[number] = jnp.where(mine, rows.astype(F32), kept_ref[number].astype(F32)).astype(BF)


def spread(flag_ref, tokens_ref, *refs):
    *received_refs, rows_ref, send_ref = refs
    rows = tokens_ref[...].astype(F32)
    for number, received_ref in enumerate(received_refs):
        here = (flag_ref[0:1, 0:1] == float(number)) & (flag_ref[1:2, 0:1] == 0.0)
        rows = jnp.where(here, received_ref[...].astype(F32), rows)
    rows = rows.astype(BF)
    rows_ref[...] = rows
    for chip in range(send_ref.shape[0]):
        send_ref[chip] = rows


def aim(pick_ref, own_ref, other_ref, goal_ref):
    pick = pick_ref[lax.axis_index("core")]
    goal_ref[...] = in_core_order(*[dot(pick, ref[...], ((1,), (1,))) for ref in (own_ref, other_ref)])


def token_errors(pick_ref, done_ref, goal_ref, send_ref):
    slices, length, cols = done_ref.shape
    pick = pick_ref[lax.axis_index("core")].astype(F32)
    total = jnp.zeros((1, pick.shape[1]), F32)
    for number in range(slices):
        span = slice(number * length, (number + 1) * length)
        diff = done_ref[number].astype(F32) - goal_ref[span, :]
        sums = jnp.sum(diff * diff, -1, keepdims=True)
        total += jnp.sum(jnp.where(pick[span] > 0.0, sums, 0.0), 0, keepdims=True)
    last = lax.axis_index("section") == lax.axis_size("section") - 1
    total = jnp.where(last, total, 0.0)
    for number in range(send_ref.shape[0]):
        send_ref[number] = total


def add_up(pieces_ref, send_ref):
    total = pieces_ref[0]
    for number in range(1, pieces_ref.shape[0]):
        total += pieces_ref[number]
    for number in range(send_ref.shape[0]):
        send_ref[number] = total


def finish_losses(pieces_ref, doc_ref, loss_ref):
    total = pieces_ref[0]
    for number in range(1, pieces_ref.shape[0]):
        total += pieces_ref[number]
    count = doc_ref.shape[1]
    mine = doc_ref[...] == iota((DOCS, count), 0)
    sums = jnp.sum(jnp.where(mine, total, 0.0), -1, keepdims=True)
    tokens = jnp.sum(jnp.where(mine, 1.0, 0.0), -1, keepdims=True)
    loss_ref[...] = jnp.broadcast_to(sums / (tokens * D), (DOCS, count))


def place_back(pick_ref, parts_ref, out_ref):
    out_ref[...] = (
        dot(pick_ref[0], parts_ref[0], ((0,), (0,))) + dot(pick_ref[1], parts_ref[1], ((0,), (0,)))
    ).astype(BF)


VMEM = pl.BlockSpec(memory_space=pltpu.VMEM)


def run(kernel, outs, *args, flops=0, bytes_accessed=1 << 16):
    several = isinstance(outs, list)
    shapes = [jax.ShapeDtypeStruct(shape, kind) for shape, kind in (outs if several else [outs])]
    return pl.pallas_call(
        kernel,
        out_shape=shapes if several else shapes[0],
        in_specs=[VMEM] * len(args),
        out_specs=[VMEM] * len(shapes) if several else VMEM,
        compiler_params=pltpu.CompilerParams(vmem_limit_bytes=24 * 1024 * 1024),
        cost_estimate=pl.CostEstimate(flops=flops, bytes_accessed=bytes_accessed, transcendentals=0),
    )(*args)


def local(tokens, targets, doc_ids, norm_gains, w_qk, w_val, w_out):
    core = lax.axis_index("core")
    sections = lax.axis_size("section")
    chips = lax.axis_size("y") * lax.axis_size("x")
    row_count, cols_own = tokens.shape
    cols = 2 * cols_own
    width = 2 * w_qk.shape[2]
    slices = 2
    length = (row_count // 2 + MOST // 2) // slices
    part = slices * length

    def swap(value):
        return lax.ppermute(value, "core", [(0, 1), (1, 0)])

    docs = doc_ids.reshape(1, row_count)
    tokens_t = jnp.swapaxes(tokens, 0, 1)
    picks, bias, first_parts, flags = run(
        prepare,
        [
            ((2, part, row_count), BF),
            ((slices, length, part), F32),
            ((slices, length, cols), BF),
            ((8, 128), F32),
        ],
        docs,
        tokens_t,
        swap(tokens_t),
    )

    keys = jnp.zeros((length, width), F32)
    vals = jnp.zeros((length, width), F32)
    done = jnp.zeros((slices, length, cols), BF)
    received = []
    goal = w_last = w_in = None
    for step in range(sections + slices - 1):
        rows, send = run(
            spread,
            [((length, cols), BF), ((chips, length, cols), BF)],
            flags,
            first_parts[min(step, slices - 1)],
            *received,
        )
        if step == 0:
            w_qk, w_val, w_out, targets, send = lax.optimization_barrier((w_qk, w_val, w_out, targets, send))
            targets_t = jnp.swapaxes(targets, 0, 1)
            targets_other = swap(targets_t)
            targets_other, w_out = lax.optimization_barrier((targets_other, jnp.swapaxes(w_out[0], 0, 1)))
            goal = run(aim, ((part, cols), F32), picks, targets_t, targets_other)
            weights = [w_qk[0], swap(w_qk[0]), w_val[0], swap(w_val[0]), w_out, swap(w_out)]
        gathered = lax.all_to_all(send, PLANE, 0, 0, tiled=True)
        if step == 0:
            w_in, w_last = pl.pallas_call(
                stage,
                out_shape=[
                    jax.ShapeDtypeStruct((D, 2 * width), BF),
                    jax.ShapeDtypeStruct((chips * width, cols), BF),
                ],
                in_specs=[pl.BlockSpec(memory_space=pltpu.HBM)] * 6,
                out_specs=[pl.BlockSpec(memory_space=pltpu.HBM)] * 2,
                scratch_shapes=[
                    pltpu.VMEM(w_out.shape, BF),
                    pltpu.VMEM(w_out.shape, BF),
                    pltpu.VMEM((D, 2 * width), BF),
                    pltpu.VMEM((chips * width, cols), BF),
                    pltpu.SemaphoreType.DMA((8,)),
                ],
                compiler_params=pltpu.CompilerParams(vmem_limit_bytes=60 * 1024 * 1024),
                cost_estimate=pl.CostEstimate(flops=0, bytes_accessed=12 * D * width, transcendentals=0),
            )(*weights)
            gathered, goal, first_parts, w_in, w_last = lax.optimization_barrier(
                (gathered, goal, first_parts, w_in, w_last)
            )
        send, keys, vals, next_flags = run(
            qkv_attention,
            [((chips, length, width), BF), ((length, width), F32), ((length, width), F32), ((8, 128), F32)],
            flags,
            gathered,
            norm_gains,
            w_in,
            bias,
            keys,
            vals,
            flops=4 * length * D * width,
            bytes_accessed=4 * D * width,
        )
        attended = lax.all_to_all(send, PLANE, 0, 0, tiled=True)
        rows, done = run(
            project_out,
            [((length, cols), BF), ((slices, length, cols), BF)],
            flags,
            attended,
            w_last,
            rows,
            done,
            flops=2 * length * chips * width * cols,
            bytes_accessed=2 * chips * width * cols,
        )
        flags = next_flags
        hops = [step - number for number in range(slices)]
        received = [
            lax.ppermute(rows, "section", [(z, z + 1)]) if 0 <= z < sections - 1 else jnp.zeros_like(rows) for z in hops
        ]

    send = run(token_errors, ((2 * chips, 1, row_count), F32), picks, done, goal)
    send = lax.all_to_all(send, PLANE + ("core",), 0, 0, tiled=True)
    send = run(add_up, ((sections, 1, row_count), F32), send)
    send = lax.all_to_all(send, "section", 0, 0, tiled=True)
    losses = run(finish_losses, ((DOCS, row_count), F32), send, docs)[:, 0]

    part_rows = done.reshape(part, cols)
    halves = [part_rows[:, :cols_own], part_rows[:, cols_own:]]
    keep = jnp.where(core == 0, halves[0], halves[1])
    other = swap(jnp.where(core == 0, halves[1], halves[0]))
    parts = jnp.stack([jnp.where(core == 0, keep, other), jnp.where(core == 0, other, keep)])
    section_rows = run(place_back, ((row_count, cols_own), BF), picks, parts)
    return (section_rows[None], losses)


def solution(mesh):
    names = ("section", "y", "x", "core")
    fine = Mesh(mesh.devices.reshape(mesh.devices.shape[0], 4, 4, 2), names)
    tensor = ("y", "x", "core")
    placed = (
        P(None, tensor),
        P(None, tensor),
        P(),
        P("section", None),
        P("section", None, tensor),
        P("section", None, tensor),
        P("section", None, tensor),
    )
    return jax.shard_map(
        local,
        mesh=fine,
        in_specs=placed,
        out_specs=(P("section", None, tensor), P()),
        check_vma=False,
    )
```

```python
import jax
import jax.numpy as jnp
from jax import lax
from jax.experimental import pallas as pl
from jax.experimental.pallas import tpu as pltpu
from jax.sharding import Mesh
from jax.sharding import PartitionSpec as P

D = 6144
HD = 64
DOCS = 8
MOST = 32
NEG = -1e30
PLANE = ("y", "x")
BF = jnp.bfloat16
F32 = jnp.float32


def iota(shape, axis):
    return lax.broadcasted_iota(jnp.int32, shape, axis)


def in_core_order(own, other):
    first = lax.axis_index("core") == 0
    return jnp.concatenate([jnp.where(first, own, other), jnp.where(first, other, own)], -1)


def dot(a, b, contract=((1,), (0,))):
    return lax.dot_general(a, b, (contract, ((), ())), preferred_element_type=F32)


def prepare(doc_ref, own_ref, other_ref, pick_ref, bias_ref, rows_ref, flag_ref):
    _, part, count = pick_ref.shape
    length = rows_ref.shape[1]
    doc_j = jnp.broadcast_to(doc_ref[...].astype(F32), (count, count))
    same = jnp.where(doc_j == jnp.transpose(doc_j), 1.0, 0.0)
    before = jnp.where(iota((count, count), 0) < iota((count, count), 1), same, 0.0)
    starts = jnp.sum(before, 0, keepdims=True) == 0.0
    lane = iota((1, count), 1)
    far = (jnp.abs(lane - count // 2) * count + lane).astype(F32)
    nearest = jnp.min(jnp.where(starts, far, float(count * count)), -1, keepdims=True)
    cut = nearest - count * jnp.floor(nearest / count)
    token = iota((part, count), 1).astype(F32)
    slot = iota((part, count), 0).astype(F32)
    picks = [
        jnp.where((token == slot) & (slot < cut), 1.0, 0.0),
        jnp.where(token == slot + cut, 1.0, 0.0),
    ]
    for core in range(2):
        pick_ref[core] = picks[core].astype(BF)
    pick = jnp.where(lax.axis_index("core") == 0, picks[0], picks[1])
    pick_bf = pick.astype(BF)
    rows = in_core_order(*[dot(pick_bf, ref[...], ((1,), (1,))) for ref in (own_ref, other_ref)])
    for number in range(part // length):
        rows_ref[number] = rows[number * length : (number + 1) * length].astype(BF)
    shifted = jnp.concatenate([jnp.zeros((length, count), F32), pick[: part - length]], 0)
    same_bf = same.astype(BF)
    for number, (queries, keys) in enumerate(((pick[:length], shifted), (pick[length:], pick))):
        alike = dot(dot(queries.astype(BF), same_bf).astype(BF), keys.astype(BF), ((1,), (1,)))
        query_at = iota((length, part), 0) + length
        key_at = iota((length, part), 1)
        allowed = ((alike > 0.5) & (key_at <= query_at)) | (key_at == query_at)
        bias_ref[number] = jnp.where(allowed, 0.0, NEG)
    section = lax.axis_index("section")
    row = iota(flag_ref.shape, 0)
    order = jnp.where(row == 0, -section, 0)
    flag_ref[...] = jnp.where((row == 1) & (section == 0), 1, order).astype(F32)


def qkv_attention(
    flag_ref,
    rows_ref,
    gain_ref,
    w_ref,
    bias_ref,
    kin_ref,
    vin_ref,
    send_ref,
    kout_ref,
    vout_ref,
    next_ref,
):
    chips, length, cols = rows_ref.shape
    width = kin_ref.shape[1]
    heads = width // HD
    total = jnp.zeros((length, cols), F32)
    for chip in range(chips):
        total += rows_ref[chip].astype(F32)
    mean = jnp.sum(total, -1, keepdims=True) / (chips * cols)
    total = jnp.zeros((length, cols), F32)
    for chip in range(chips):
        centered = rows_ref[chip].astype(F32) - mean
        total += centered * centered
    scale = lax.rsqrt(jnp.sum(total, -1, keepdims=True) / (chips * cols) + 1e-05)
    acc = jnp.zeros((length, 2 * width), F32)
    for chip in range(chips):
        span = slice(chip * cols, (chip + 1) * cols)
        centered = rows_ref[chip].astype(F32) - mean
        normed = (centered * scale * gain_ref[:, span]).astype(BF)
        acc += dot(normed, w_ref[span, :])
    rounded = acc.astype(BF).astype(F32)
    qk, val = rounded[:, :width], rounded[:, width:]
    head_of = iota((length, width), 1) // HD
    squares = qk * qk
    inverse = jnp.zeros((length, width), F32)
    stack = []
    for head in range(heads):
        mine = head_of == head
        square_mean = jnp.sum(jnp.where(mine, squares, 0.0), -1, keepdims=True) / HD
        inverse = jnp.where(mine, lax.rsqrt(square_mean + 1e-06), inverse)
        stack.append(jnp.where(mine, qk, 0.0))
    key = (qk * inverse).astype(BF).astype(F32)
    queries = jnp.concatenate(stack, 0).astype(BF)
    keys = jnp.concatenate([kin_ref[...], key], 0).astype(BF)
    vals = jnp.concatenate([vin_ref[...], val], 0).astype(BF)
    bias = jnp.where(flag_ref[0:1, 0:1] > 0.0, bias_ref[1], bias_ref[0])
    scores = dot(queries, keys, ((1,), (1,))) / HD + jnp.concatenate([bias] * heads, 0)
    peak = jnp.max(scores, -1, keepdims=True)
    expo = jnp.exp(scores - peak)
    weights = (expo / jnp.sum(expo, -1, keepdims=True)).astype(BF)
    mixed = dot(weights, vals)
    attended = jnp.zeros((length, width), F32)
    for head in range(heads):
        attended = jnp.where(head_of == head, mixed[head * length : (head + 1) * length], attended)
    half = width // 2
    attended = in_core_order(attended[:, :half], attended[:, half:]).astype(BF)
    for chip in range(chips):
        send_ref[chip] = attended
    kout_ref[...] = key
    vout_ref[...] = val
    next_ref[...] = flag_ref[...] + jnp.where(iota(flag_ref.shape, 0) == 0, 1.0, 0.0)


def stage(qk_ref, qk_other_ref, val_ref, val_other_ref, out_ref, out_other_ref, in_ref, last_ref, *scratch):
    own, other, packed, turned, sems = scratch
    width = qk_ref.shape[1]
    copies = [(out_ref, own), (out_other_ref, other)]
    for number, ref in enumerate((qk_ref, qk_other_ref, val_ref, val_other_ref)):
        copies.append((ref, packed.at[:, pl.ds(number * width, width)]))
    copies += [(packed, in_ref), (turned, last_ref)]
    copies = [pltpu.make_async_copy(*pair, sems.at[number]) for number, pair in enumerate(copies)]
    for copy in copies[:6]:
        copy.start()
    for copy in copies[:6]:
        copy.wait()
    copies[6].start()
    block = 256
    first = lax.axis_index("core") == 0
    for begin in range(0, own.shape[1], block):
        span = slice(begin, begin + block)
        here, there = own[:, span], other[:, span]
        here, there = jnp.where(first, here, there), jnp.where(first, there, here)
        turned[span, :] = jnp.transpose(jnp.concatenate([here, there], 0))
    copies[7].start()
    copies[6].wait()
    copies[7].wait()


def project_out(flag_ref, heads_ref, w_ref, rows_ref, kept_ref, out_ref, done_ref):
    chips, _, width = heads_ref.shape
    mixed = jnp.zeros(rows_ref.shape, F32)
    for chip in range(chips):
        mixed += dot(heads_ref[chip], w_ref[chip * width : (chip + 1) * width, :])
    rows = (rows_ref[...].astype(F32) + mixed).astype(BF)
    out_ref[...] = rows
    for number in range(kept_ref.shape[0]):
        mine = flag_ref[0:1, 0:1] == float(number)
        done_ref[number] = jnp.where(mine, rows.astype(F32), kept_ref[number].astype(F32)).astype(BF)


def spread(flag_ref, tokens_ref, *refs):
    *received_refs, rows_ref, send_ref = refs
    rows = tokens_ref[...].astype(F32)
    for number, received_ref in enumerate(reversed(received_refs)):
        here = (flag_ref[0:1, 0:1] == float(number)) & (flag_ref[1:2, 0:1] == 0.0)
        rows = jnp.where(here, received_ref[...].astype(F32), rows)
    rows = rows.astype(BF)
    rows_ref[...] = rows
    for chip in range(send_ref.shape[0]):
        send_ref[chip] = rows


def aim(pick_ref, own_ref, other_ref, goal_ref):
    pick = pick_ref[lax.axis_index("core")]
    goal_ref[...] = in_core_order(*[dot(pick, ref[...], ((1,), (1,))) for ref in (own_ref, other_ref)])


def token_errors(pick_ref, done_ref, goal_ref, send_ref):
    slices, length, cols = done_ref.shape
    pick = pick_ref[lax.axis_index("core")].astype(F32)
    total = jnp.zeros((1, pick.shape[1]), F32)
    for number in range(slices):
        span = slice(number * length, (number + 1) * length)
        diff = done_ref[number].astype(F32) - goal_ref[span, :]
        sums = jnp.sum(diff * diff, -1, keepdims=True)
        total += jnp.sum(jnp.where(pick[span] > 0.0, sums, 0.0), 0, keepdims=True)
    last = lax.axis_index("section") == lax.axis_size("section") - 1
    total = jnp.where(last, total, 0.0)
    for number in range(send_ref.shape[0]):
        send_ref[number] = total


def add_up(pieces_ref, send_ref):
    total = pieces_ref[0]
    for number in range(1, pieces_ref.shape[0]):
        total += pieces_ref[number]
    for number in range(send_ref.shape[0]):
        send_ref[number] = total


def finish_losses(pieces_ref, doc_ref, loss_ref):
    total = pieces_ref[0]
    for number in range(1, pieces_ref.shape[0]):
        total += pieces_ref[number]
    count = doc_ref.shape[1]
    mine = doc_ref[...] == iota((DOCS, count), 0)
    sums = jnp.sum(jnp.where(mine, total, 0.0), -1, keepdims=True)
    tokens = jnp.sum(jnp.where(mine, 1.0, 0.0), -1, keepdims=True)
    loss_ref[...] = jnp.broadcast_to(sums / (tokens * D), (DOCS, count))


def place_back(pick_ref, parts_ref, out_ref):
    out_ref[...] = (
        dot(pick_ref[0], parts_ref[0], ((0,), (0,))) + dot(pick_ref[1], parts_ref[1], ((0,), (0,)))
    ).astype(BF)


VMEM = pl.BlockSpec(memory_space=pltpu.VMEM)


def run(kernel, outs, *args, flops=0, bytes_accessed=1 << 16):
    several = isinstance(outs, list)
    shapes = [jax.ShapeDtypeStruct(shape, kind) for shape, kind in (outs if several else [outs])]
    return pl.pallas_call(
        kernel,
        out_shape=shapes if several else shapes[0],
        in_specs=[VMEM] * len(args),
        out_specs=[VMEM] * len(shapes) if several else VMEM,
        compiler_params=pltpu.CompilerParams(vmem_limit_bytes=24 * 1024 * 1024),
        cost_estimate=pl.CostEstimate(flops=flops, bytes_accessed=bytes_accessed, transcendentals=0),
    )(*args)


def local(tokens, targets, doc_ids, norm_gains, w_qk, w_val, w_out):
    core = lax.axis_index("core")
    sections = lax.axis_size("section")
    chips = lax.axis_size("y") * lax.axis_size("x")
    row_count, cols_own = tokens.shape
    cols = 2 * cols_own
    width = 2 * w_qk.shape[2]
    slices = 2
    length = (row_count // 2 + MOST // 2) // slices
    part = slices * length

    def swap(value):
        return lax.ppermute(value, "core", [(0, 1), (1, 0)])

    docs = doc_ids.reshape(1, row_count)
    tokens_t = jnp.swapaxes(tokens, 0, 1)
    picks, bias, first_parts, flags = run(
        prepare,
        [
            ((2, part, row_count), BF),
            ((slices, length, part), F32),
            ((slices, length, cols), BF),
            ((8, 128), F32),
        ],
        docs,
        tokens_t,
        swap(tokens_t),
    )

    keys = jnp.zeros((length, width), F32)
    vals = jnp.zeros((length, width), F32)
    done = jnp.zeros((slices, length, cols), BF)
    received = []
    goal = w_last = w_in = None
    for step in range(sections + slices - 1):
        rows, send = run(
            spread,
            [((length, cols), BF), ((chips, length, cols), BF)],
            flags,
            first_parts[min(step, slices - 1)],
            *reversed(received),
        )
        if step == 0:
            w_qk, w_val, w_out, send = lax.optimization_barrier((w_qk, w_val, w_out, send))
            w_out = jnp.swapaxes(w_out[0], 0, 1)
            weights = [w_qk[0], swap(w_qk[0]), w_val[0], swap(w_val[0]), w_out, swap(w_out)]
        gathered = lax.all_to_all(send, PLANE, 0, 0, tiled=True)
        if step == 0:
            w_in, w_last = pl.pallas_call(
                stage,
                out_shape=[
                    jax.ShapeDtypeStruct((D, 2 * width), BF),
                    jax.ShapeDtypeStruct((chips * width, cols), BF),
                ],
                in_specs=[pl.BlockSpec(memory_space=pltpu.HBM)] * 6,
                out_specs=[pl.BlockSpec(memory_space=pltpu.HBM)] * 2,
                scratch_shapes=[
                    pltpu.VMEM(w_out.shape, BF),
                    pltpu.VMEM(w_out.shape, BF),
                    pltpu.VMEM((D, 2 * width), BF),
                    pltpu.VMEM((chips * width, cols), BF),
                    pltpu.SemaphoreType.DMA((8,)),
                ],
                compiler_params=pltpu.CompilerParams(vmem_limit_bytes=60 * 1024 * 1024),
                cost_estimate=pl.CostEstimate(flops=0, bytes_accessed=12 * D * width, transcendentals=0),
            )(*weights)
            gathered, first_parts, w_in, w_last = lax.optimization_barrier((gathered, first_parts, w_in, w_last))
        send, keys, vals, next_flags = run(
            qkv_attention,
            [((chips, length, width), BF), ((length, width), F32), ((length, width), F32), ((8, 128), F32)],
            flags,
            gathered,
            norm_gains,
            w_in,
            bias,
            keys,
            vals,
            flops=4 * length * D * width,
            bytes_accessed=4 * D * width,
        )
        attended = lax.all_to_all(send, PLANE, 0, 0, tiled=True)
        if step == sections + slices - 2:
            attended, picks, goal = lax.optimization_barrier((attended, picks, goal))
        rows, done = run(
            project_out,
            [((length, cols), BF), ((slices, length, cols), BF)],
            flags,
            attended,
            w_last,
            rows,
            done,
            flops=2 * length * chips * width * cols,
            bytes_accessed=2 * chips * width * cols,
        )
        flags = next_flags
        received = {}
        for number in reversed(range(slices)):
            z = step - number
            if 0 <= z < sections - 1:
                received[number] = lax.ppermute(rows, "section", [(z, z + 1)])
            else:
                received[number] = jnp.zeros_like(rows)
        received = [received[number] for number in range(slices)]
        if step == sections // 2:
            targets, rows = lax.optimization_barrier((targets, rows))
            targets_t = jnp.swapaxes(targets, 0, 1)
            goal = run(aim, ((part, cols), F32), picks, targets_t, swap(targets_t))
            goal, picks, received = lax.optimization_barrier((goal, picks, received))

    send = run(token_errors, ((2 * chips, 1, row_count), F32), picks, done, goal)
    send = lax.all_to_all(send, PLANE + ("core",), 0, 0, tiled=True)
    send, done = lax.optimization_barrier((send, done))
    send = run(add_up, ((sections, 1, row_count), F32), send)
    send = lax.all_to_all(send, "section", 0, 0, tiled=True)
    losses = run(finish_losses, ((DOCS, row_count), F32), send, docs)[:, 0]

    part_rows = done.reshape(part, cols)
    halves = [part_rows[:, :cols_own], part_rows[:, cols_own:]]
    keep = jnp.where(core == 0, halves[0], halves[1])
    other = swap(jnp.where(core == 0, halves[1], halves[0]))
    parts = jnp.stack([jnp.where(core == 0, keep, other), jnp.where(core == 0, other, keep)])
    section_rows = run(place_back, ((row_count, cols_own), BF), picks, parts)
    return (section_rows[None], losses)


def solution(mesh):
    names = ("section", "y", "x", "core")
    fine = Mesh(mesh.devices.reshape(mesh.devices.shape[0], 4, 4, 2), names)
    tensor = ("y", "x", "core")
    placed = (
        P(None, tensor),
        P(None, tensor),
        P(),
        P("section", None),
        P("section", None, tensor),
        P("section", None, tensor),
        P("section", None, tensor),
    )
    return jax.shard_map(
        local,
        mesh=fine,
        in_specs=placed,
        out_specs=(P("section", None, tensor), P()),
        check_vma=False,
    )
```

```python
import functools

import jax
import jax.numpy as jnp
from jax import lax
from jax.experimental import pallas as pl
from jax.experimental.pallas import tpu as pltpu
from jax.sharding import Mesh
from jax.sharding import PartitionSpec as P

D = 6144
HD = 64
DOCS = 8
MOST = 32
NEG = -1e30
PLANE = ("y", "x")
BF = jnp.bfloat16
F32 = jnp.float32


def iota(shape, axis):
    return lax.broadcasted_iota(jnp.int32, shape, axis)


def in_core_order(own, other):
    first = lax.axis_index("core") == 0
    return jnp.concatenate([jnp.where(first, own, other), jnp.where(first, other, own)], -1)


def dot(a, b, contract=((1,), (0,))):
    return lax.dot_general(a, b, (contract, ((), ())), preferred_element_type=F32)


def prepare(doc_ref, own_ref, other_ref, pick_ref, bias_ref, rows_ref, flag_ref):
    _, part, count = pick_ref.shape
    length = rows_ref.shape[1]
    doc_j = jnp.broadcast_to(doc_ref[...].astype(F32), (count, count))
    same = jnp.where(doc_j == jnp.transpose(doc_j), 1.0, 0.0)
    before = jnp.where(iota((count, count), 0) < iota((count, count), 1), same, 0.0)
    starts = jnp.sum(before, 0, keepdims=True) == 0.0
    lane = iota((1, count), 1)
    far = (jnp.abs(lane - count // 2) * count + lane).astype(F32)
    nearest = jnp.min(jnp.where(starts, far, float(count * count)), -1, keepdims=True)
    cut = nearest - count * jnp.floor(nearest / count)
    token = iota((part, count), 1).astype(F32)
    slot = iota((part, count), 0).astype(F32)
    picks = [
        jnp.where((token == slot) & (slot < cut), 1.0, 0.0),
        jnp.where(token == slot + cut, 1.0, 0.0),
    ]
    for core in range(2):
        pick_ref[core] = picks[core].astype(BF)
    pick = jnp.where(lax.axis_index("core") == 0, picks[0], picks[1])
    pick_bf = pick.astype(BF)
    rows = in_core_order(*[dot(pick_bf, ref[...], ((1,), (1,))) for ref in (own_ref, other_ref)])
    for number in range(part // length):
        rows_ref[number] = rows[number * length : (number + 1) * length].astype(BF)
    shifted = jnp.concatenate([jnp.zeros((length, count), F32), pick[: part - length]], 0)
    same_bf = same.astype(BF)
    for number, (queries, keys) in enumerate(((pick[:length], shifted), (pick[length:], pick))):
        alike = dot(dot(queries.astype(BF), same_bf).astype(BF), keys.astype(BF), ((1,), (1,)))
        query_at = iota((length, part), 0) + length
        key_at = iota((length, part), 1)
        allowed = ((alike > 0.5) & (key_at <= query_at)) | (key_at == query_at)
        bias_ref[number] = jnp.where(allowed, 0.0, NEG)
    section = lax.axis_index("section")
    row = iota(flag_ref.shape, 0)
    order = jnp.where(row == 0, -section, 0)
    flag_ref[...] = jnp.where((row == 1) & (section == 0), 1, order).astype(F32)


def qkv_attention(
    flag_ref,
    rows_ref,
    gain_ref,
    w_ref,
    bias_ref,
    kin_ref,
    vin_ref,
    send_ref,
    kout_ref,
    vout_ref,
    next_ref,
):
    chips, length, cols = rows_ref.shape
    width = kin_ref.shape[1]
    heads = width // HD
    total = jnp.zeros((length, cols), F32)
    for chip in range(chips):
        total += rows_ref[chip].astype(F32)
    mean = jnp.sum(total, -1, keepdims=True) / (chips * cols)
    total = jnp.zeros((length, cols), F32)
    for chip in range(chips):
        centered = rows_ref[chip].astype(F32) - mean
        total += centered * centered
    scale = lax.rsqrt(jnp.sum(total, -1, keepdims=True) / (chips * cols) + 1e-05)
    acc = jnp.zeros((length, 2 * width), F32)
    for pair in range(0, chips, 2):
        normed = []
        for chip in (pair, pair + 1):
            centered = rows_ref[chip].astype(F32) - mean
            normed.append((centered * scale * gain_ref[:, chip * cols : (chip + 1) * cols]).astype(BF))
        acc += dot(jnp.concatenate(normed, 1), w_ref[pair * cols : (pair + 2) * cols, :])
    rounded = acc.astype(BF).astype(F32)
    qk, val = rounded[:, :width], rounded[:, width:]
    head_of = iota((length, width), 1) // HD
    squares = qk * qk
    inverse = jnp.zeros((length, width), F32)
    stack = []
    for head in range(heads):
        mine = head_of == head
        square_mean = jnp.sum(jnp.where(mine, squares, 0.0), -1, keepdims=True) / HD
        inverse = jnp.where(mine, lax.rsqrt(square_mean + 1e-06), inverse)
        stack.append(jnp.where(mine, qk, 0.0))
    key = (qk * inverse).astype(BF).astype(F32)
    queries = jnp.concatenate(stack, 0).astype(BF)
    keys = jnp.concatenate([kin_ref[...], key], 0).astype(BF)
    vals = jnp.concatenate([vin_ref[...], val], 0).astype(BF)
    bias = jnp.where(flag_ref[0:1, 0:1] > 0.0, bias_ref[1], bias_ref[0])
    scores = dot(queries, keys, ((1,), (1,))) / HD + jnp.concatenate([bias] * heads, 0)
    peak = jnp.max(scores, -1, keepdims=True)
    expo = jnp.exp(scores - peak)
    weights = (expo / jnp.sum(expo, -1, keepdims=True)).astype(BF)
    mixed = dot(weights, vals)
    attended = jnp.zeros((length, width), F32)
    for head in range(heads):
        attended = jnp.where(head_of == head, mixed[head * length : (head + 1) * length], attended)
    half = width // 2
    attended = in_core_order(attended[:, :half], attended[:, half:]).astype(BF)
    for chip in range(chips):
        send_ref[chip] = attended
    kout_ref[...] = key
    vout_ref[...] = val
    next_ref[...] = flag_ref[...] + jnp.where(iota(flag_ref.shape, 0) == 0, 1.0, 0.0)


def stage(qk_ref, qk_other_ref, val_ref, val_other_ref, out_ref, out_other_ref, in_ref, last_ref, *scratch):
    own, other, packed, turned, sems = scratch
    width = qk_ref.shape[1]
    copies = [(out_ref, own), (out_other_ref, other)]
    for number, ref in enumerate((qk_ref, qk_other_ref, val_ref, val_other_ref)):
        copies.append((ref, packed.at[:, pl.ds(number * width, width)]))
    copies += [(packed, in_ref), (turned, last_ref)]
    copies = [pltpu.make_async_copy(*pair, sems.at[number]) for number, pair in enumerate(copies)]
    for copy in copies[:6]:
        copy.start()
    for copy in copies[:6]:
        copy.wait()
    copies[6].start()
    block = 256
    first = lax.axis_index("core") == 0
    for begin in range(0, own.shape[1], block):
        span = slice(begin, begin + block)
        here, there = own[:, span], other[:, span]
        here, there = jnp.where(first, here, there), jnp.where(first, there, here)
        turned[span, :] = jnp.transpose(jnp.concatenate([here, there], 0))
    copies[7].start()
    copies[6].wait()
    copies[7].wait()


def project_out(flag_ref, heads_ref, w_ref, rows_ref, kept_ref, out_ref, done_ref):
    chips, _, width = heads_ref.shape
    mixed = jnp.zeros(rows_ref.shape, F32)
    for chip in range(chips):
        mixed += dot(heads_ref[chip], w_ref[chip * width : (chip + 1) * width, :])
    rows = (rows_ref[...].astype(F32) + mixed).astype(BF)
    out_ref[...] = rows
    for number in range(kept_ref.shape[0]):
        mine = flag_ref[0:1, 0:1] == float(number)
        done_ref[number] = jnp.where(mine, rows.astype(F32), kept_ref[number].astype(F32)).astype(BF)


def spread(backward, flag_ref, tokens_ref, *refs):
    *received_refs, rows_ref, send_ref = refs
    received_refs = list(enumerate(reversed(received_refs) if backward else received_refs))
    rows = tokens_ref[...].astype(F32)
    for number, received_ref in received_refs:
        here = (flag_ref[0:1, 0:1] == float(number)) & (flag_ref[1:2, 0:1] == 0.0)
        rows = jnp.where(here, received_ref[...].astype(F32), rows)
    rows = rows.astype(BF)
    rows_ref[...] = rows
    for chip in range(send_ref.shape[0]):
        send_ref[chip] = rows


def row_parts(keep_ref, other_ref):
    first = lax.axis_index("core") == 0
    keep, other = keep_ref[...], other_ref[...]
    return jnp.where(first, keep, other), jnp.where(first, other, keep)


def token_errors(pick_ref, keep_ref, other_ref, targets_ref, send_ref):
    parts = row_parts(keep_ref, other_ref)
    rows = dot(parts[0], pick_ref[0], ((0,), (0,))) + dot(parts[1], pick_ref[1], ((0,), (0,)))
    diff = rows - targets_ref[...].astype(F32)
    total = jnp.sum(diff * diff, 0, keepdims=True)
    last = lax.axis_index("section") == lax.axis_size("section") - 1
    total = jnp.where(last, total, 0.0)
    for number in range(send_ref.shape[0]):
        send_ref[number] = total


def add_up(pieces_ref, send_ref):
    total = pieces_ref[0]
    for number in range(1, pieces_ref.shape[0]):
        total += pieces_ref[number]
    for number in range(send_ref.shape[0]):
        send_ref[number] = total


def finish_losses(pieces_ref, doc_ref, loss_ref):
    total = pieces_ref[0]
    for number in range(1, pieces_ref.shape[0]):
        total += pieces_ref[number]
    count = doc_ref.shape[1]
    mine = doc_ref[...] == iota((DOCS, count), 0)
    sums = jnp.sum(jnp.where(mine, total, 0.0), -1, keepdims=True)
    tokens = jnp.sum(jnp.where(mine, 1.0, 0.0), -1, keepdims=True)
    loss_ref[...] = jnp.broadcast_to(sums / (tokens * D), (DOCS, count))


def place_back(pick_ref, keep_ref, other_ref, out_ref):
    parts = row_parts(keep_ref, other_ref)
    out_ref[...] = (
        dot(pick_ref[0], parts[0], ((0,), (0,))) + dot(pick_ref[1], parts[1], ((0,), (0,)))
    ).astype(BF)


VMEM = pl.BlockSpec(memory_space=pltpu.VMEM)


def run(kernel, outs, *args, flops=0, bytes_accessed=1 << 16):
    several = isinstance(outs, list)
    shapes = [jax.ShapeDtypeStruct(shape, kind) for shape, kind in (outs if several else [outs])]
    return pl.pallas_call(
        kernel,
        out_shape=shapes if several else shapes[0],
        in_specs=[VMEM] * len(args),
        out_specs=[VMEM] * len(shapes) if several else VMEM,
        compiler_params=pltpu.CompilerParams(vmem_limit_bytes=24 * 1024 * 1024),
        cost_estimate=pl.CostEstimate(flops=flops, bytes_accessed=bytes_accessed, transcendentals=0),
    )(*args)


def local(tokens, targets, doc_ids, norm_gains, w_qk, w_val, w_out):
    core = lax.axis_index("core")
    sections = lax.axis_size("section")
    chips = lax.axis_size("y") * lax.axis_size("x")
    row_count, cols_own = tokens.shape
    cols = 2 * cols_own
    width = 2 * w_qk.shape[2]
    slices = 2
    length = (row_count // 2 + MOST // 2) // slices
    part = slices * length

    def swap(value):
        return lax.ppermute(value, "core", [(0, 1), (1, 0)])

    docs = doc_ids.reshape(1, row_count)
    tokens_t = jnp.swapaxes(tokens, 0, 1)
    picks, bias, first_parts, flags = run(
        prepare,
        [
            ((2, part, row_count), BF),
            ((slices, length, part), F32),
            ((slices, length, cols), BF),
            ((8, 128), F32),
        ],
        docs,
        tokens_t,
        swap(tokens_t),
    )

    keys = jnp.zeros((length, width), F32)
    vals = jnp.zeros((length, width), F32)
    done = jnp.zeros((slices, length, cols), BF)
    received = []
    w_last = w_in = None
    for step in range(sections + slices - 1):
        backward = step % 2 == 1
        rows, send = run(
            functools.partial(spread, backward),
            [((length, cols), BF), ((chips, length, cols), BF)],
            flags,
            first_parts[min(step, slices - 1)],
            *(reversed(received) if backward else received),
        )
        if step == 0:
            w_qk, w_val, w_out, send = lax.optimization_barrier((w_qk, w_val, w_out, send))
            w_out = jnp.swapaxes(w_out[0], 0, 1)
            weights = [w_qk[0], swap(w_qk[0]), w_val[0], swap(w_val[0]), w_out, swap(w_out)]
        gathered = lax.all_to_all(send, PLANE, 0, 0, tiled=True)
        if step == 0:
            w_in, w_last = pl.pallas_call(
                stage,
                out_shape=[
                    jax.ShapeDtypeStruct((D, 2 * width), BF),
                    jax.ShapeDtypeStruct((chips * width, cols), BF),
                ],
                in_specs=[pl.BlockSpec(memory_space=pltpu.HBM)] * 6,
                out_specs=[pl.BlockSpec(memory_space=pltpu.HBM)] * 2,
                scratch_shapes=[
                    pltpu.VMEM(w_out.shape, BF),
                    pltpu.VMEM(w_out.shape, BF),
                    pltpu.VMEM((D, 2 * width), BF),
                    pltpu.VMEM((chips * width, cols), BF),
                    pltpu.SemaphoreType.DMA((8,)),
                ],
                compiler_params=pltpu.CompilerParams(vmem_limit_bytes=60 * 1024 * 1024),
                cost_estimate=pl.CostEstimate(flops=0, bytes_accessed=12 * D * width, transcendentals=0),
            )(*weights)
            gathered, first_parts, w_in, w_last = lax.optimization_barrier((gathered, first_parts, w_in, w_last))
        send, keys, vals, next_flags = run(
            qkv_attention,
            [((chips, length, width), BF), ((length, width), F32), ((length, width), F32), ((8, 128), F32)],
            flags,
            gathered,
            norm_gains,
            w_in,
            bias,
            keys,
            vals,
            flops=4 * length * D * width,
            bytes_accessed=4 * D * width,
        )
        attended = lax.all_to_all(send, PLANE, 0, 0, tiled=True)
        if step == sections + slices - 2:
            attended, picks, targets = lax.optimization_barrier((attended, picks, targets))
        rows, done = run(
            project_out,
            [((length, cols), BF), ((slices, length, cols), BF)],
            flags,
            attended,
            w_last,
            rows,
            done,
            flops=2 * length * chips * width * cols,
            bytes_accessed=2 * chips * width * cols,
        )
        flags = next_flags
        received = {}
        for number in reversed(range(slices)):
            z = step - number
            if 0 <= z < sections - 1:
                received[number] = lax.ppermute(rows, "section", [(z, z + 1)])
            else:
                received[number] = jnp.zeros_like(rows)
        received = [received[number] for number in range(slices)]

    part_rows = done.reshape(part, cols)
    halves = [part_rows[:, :cols_own], part_rows[:, cols_own:]]
    keep = jnp.where(core == 0, halves[0], halves[1])
    other = swap(jnp.where(core == 0, halves[1], halves[0]))
    targets_t = jnp.swapaxes(targets, 0, 1)
    send = run(token_errors, ((2 * chips, 1, row_count), F32), picks, keep, other, targets_t)
    send = lax.all_to_all(send, PLANE + ("core",), 0, 0, tiled=True)
    send = run(add_up, ((sections, 1, row_count), F32), send)
    send = lax.all_to_all(send, "section", 0, 0, tiled=True)
    losses = run(finish_losses, ((DOCS, row_count), F32), send, docs)[:, 0]

    section_rows = run(place_back, ((row_count, cols_own), BF), picks, keep, other)
    return (section_rows[None], losses)


def solution(mesh):
    names = ("section", "y", "x", "core")
    fine = Mesh(mesh.devices.reshape(mesh.devices.shape[0], 4, 4, 2), names)
    tensor = ("y", "x", "core")
    placed = (
        P(None, tensor),
        P(None, tensor),
        P(),
        P("section", None),
        P("section", None, tensor),
        P("section", None, tensor),
        P("section", None, tensor),
    )
    return jax.shard_map(
        local,
        mesh=fine,
        in_specs=placed,
        out_specs=(P("section", None, tensor), P()),
        check_vma=False,
    )
```

```python
import functools

import jax
import jax.numpy as jnp
from jax import lax
from jax.experimental import pallas as pl
from jax.experimental.pallas import tpu as pltpu
from jax.sharding import Mesh
from jax.sharding import PartitionSpec as P

D = 6144
HD = 64
DOCS = 8
MOST = 32
NEG = -1e30
PLANE = ("y", "x")
BF = jnp.bfloat16
F32 = jnp.float32


def iota(shape, axis):
    return lax.broadcasted_iota(jnp.int32, shape, axis)


def in_core_order(own, other):
    first = lax.axis_index("core") == 0
    return jnp.concatenate([jnp.where(first, own, other), jnp.where(first, other, own)], -1)


def dot(a, b, contract=((1,), (0,))):
    return lax.dot_general(a, b, (contract, ((), ())), preferred_element_type=F32)


def prepare(doc_ref, own_ref, other_ref, pick_ref, bias_ref, rows_ref, flag_ref):
    _, part, count = pick_ref.shape
    length = rows_ref.shape[1]
    doc_j = jnp.broadcast_to(doc_ref[...].astype(F32), (count, count))
    same = jnp.where(doc_j == jnp.transpose(doc_j), 1.0, 0.0)
    before = jnp.where(iota((count, count), 0) < iota((count, count), 1), same, 0.0)
    starts = jnp.sum(before, 0, keepdims=True) == 0.0
    lane = iota((1, count), 1)
    far = (jnp.abs(lane - count // 2) * count + lane).astype(F32)
    nearest = jnp.min(jnp.where(starts, far, float(count * count)), -1, keepdims=True)
    cut = nearest - count * jnp.floor(nearest / count)
    token = iota((part, count), 1).astype(F32)
    slot = iota((part, count), 0).astype(F32)
    picks = [
        jnp.where((token == slot) & (slot < cut), 1.0, 0.0),
        jnp.where(token == slot + cut, 1.0, 0.0),
    ]
    for core in range(2):
        pick_ref[core] = picks[core].astype(BF)
    pick = jnp.where(lax.axis_index("core") == 0, picks[0], picks[1])
    pick_bf = pick.astype(BF)
    rows = in_core_order(*[dot(pick_bf, ref[...], ((1,), (1,))) for ref in (own_ref, other_ref)])
    for number in range(part // length):
        rows_ref[number] = rows[number * length : (number + 1) * length].astype(BF)
    shifted = jnp.concatenate([jnp.zeros((length, count), F32), pick[: part - length]], 0)
    same_bf = same.astype(BF)
    for number, (queries, keys) in enumerate(((pick[:length], shifted), (pick[length:], pick))):
        alike = dot(dot(queries.astype(BF), same_bf).astype(BF), keys.astype(BF), ((1,), (1,)))
        query_at = iota((length, part), 0) + length
        key_at = iota((length, part), 1)
        allowed = ((alike > 0.5) & (key_at <= query_at)) | (key_at == query_at)
        bias_ref[number] = jnp.where(allowed, 0.0, NEG)
    section = lax.axis_index("section")
    row = iota(flag_ref.shape, 0)
    order = jnp.where(row == 0, -section, 0)
    order = jnp.where((row == 1) & (section == 0), 1, order)
    flag_ref[...] = jnp.where(row == 2, lax.axis_index("core"), order).astype(F32)


def qkv_attention(
    flag_ref,
    rows_ref,
    gain_ref,
    w_ref,
    bias_ref,
    kin_ref,
    vin_ref,
    send_ref,
    kout_ref=None,
    vout_ref=None,
    next_ref=None,
):
    chips, length, cols = rows_ref.shape
    width = kin_ref.shape[1]
    heads = width // HD
    total = jnp.zeros((length, cols), F32)
    for chip in range(chips):
        total += rows_ref[chip].astype(F32)
    mean = jnp.sum(total, -1, keepdims=True) / (chips * cols)
    total = jnp.zeros((length, cols), F32)
    for chip in range(chips):
        centered = rows_ref[chip].astype(F32) - mean
        total += centered * centered
    scale = lax.rsqrt(jnp.sum(total, -1, keepdims=True) / (chips * cols) + 1e-05)
    acc = jnp.zeros((length, 2 * width), F32)
    for pair in range(0, chips, 2):
        normed = []
        for chip in (pair, pair + 1):
            centered = rows_ref[chip].astype(F32) - mean
            normed.append((centered * scale * gain_ref[:, chip * cols : (chip + 1) * cols]).astype(BF))
        acc += dot(jnp.concatenate(normed, 1), w_ref[pair * cols : (pair + 2) * cols, :])
    rounded = acc.astype(BF).astype(F32)
    qk, val = rounded[:, :width], rounded[:, width:]
    head_of = iota((length, width), 1) // HD
    squares = qk * qk
    inverse = jnp.zeros((length, width), F32)
    stack = []
    for head in range(heads):
        mine = head_of == head
        square_mean = jnp.sum(jnp.where(mine, squares, 0.0), -1, keepdims=True) / HD
        inverse = jnp.where(mine, lax.rsqrt(square_mean + 1e-06), inverse)
        stack.append(jnp.where(mine, qk, 0.0))
    key = (qk * inverse).astype(BF).astype(F32)
    queries = jnp.concatenate(stack, 0).astype(BF)
    keys = jnp.concatenate([kin_ref[...], key], 0).astype(BF)
    vals = jnp.concatenate([vin_ref[...], val], 0).astype(BF)
    bias = jnp.where(flag_ref[0:1, 0:1] > 0.0, bias_ref[1], bias_ref[0])
    scores = dot(queries, keys, ((1,), (1,))) / HD + jnp.concatenate([bias] * heads, 0)
    peak = jnp.max(scores, -1, keepdims=True)
    expo = jnp.exp(scores - peak)
    weights = (expo / jnp.sum(expo, -1, keepdims=True)).astype(BF)
    mixed = dot(weights, vals)
    attended = jnp.zeros((length, width), F32)
    for head in range(heads):
        attended = jnp.where(head_of == head, mixed[head * length : (head + 1) * length], attended)
    half = width // 2
    attended = in_core_order(attended[:, :half], attended[:, half:]).astype(BF)
    for chip in range(chips):
        send_ref[chip] = attended
    if kout_ref is None:
        return
    kout_ref[...] = key
    vout_ref[...] = val
    next_ref[...] = flag_ref[...] + jnp.where(iota(flag_ref.shape, 0) == 0, 1.0, 0.0)


def stage(qk_ref, qk_other_ref, val_ref, val_other_ref, out_ref, out_other_ref, in_ref, last_ref, *scratch):
    own, other, packed, turned, sems = scratch
    width = qk_ref.shape[1]
    copies = [(out_ref, own), (out_other_ref, other)]
    for number, ref in enumerate((qk_ref, qk_other_ref, val_ref, val_other_ref)):
        copies.append((ref, packed.at[:, pl.ds(number * width, width)]))
    copies += [(packed, in_ref), (turned, last_ref)]
    copies = [pltpu.make_async_copy(*pair, sems.at[number]) for number, pair in enumerate(copies)]
    for copy in copies[:6]:
        copy.start()
    for copy in copies[:6]:
        copy.wait()
    copies[6].start()
    block = 256
    first = lax.axis_index("core") == 0
    for begin in range(0, own.shape[1], block):
        span = slice(begin, begin + block)
        here, there = own[:, span], other[:, span]
        here, there = jnp.where(first, here, there), jnp.where(first, there, here)
        turned[span, :] = jnp.transpose(jnp.concatenate([here, there], 0))
    copies[7].start()
    copies[6].wait()
    copies[7].wait()


def project_out(flag_ref, heads_ref, w_ref, rows_ref, kept_ref, done_ref, out_ref=None):
    chips, _, width = heads_ref.shape
    mixed = jnp.zeros(rows_ref.shape, F32)
    for chip in range(chips):
        mixed += dot(heads_ref[chip], w_ref[chip * width : (chip + 1) * width, :])
    rows = (rows_ref[...].astype(F32) + mixed).astype(BF)
    if out_ref is not None:
        out_ref[...] = rows
    for number in range(kept_ref.shape[0]):
        mine = flag_ref[0:1, 0:1] == float(number)
        done_ref[number] = jnp.where(mine, rows.astype(F32), kept_ref[number].astype(F32)).astype(BF)


def spread(backward, flag_ref, tokens_ref, *refs):
    *received_refs, rows_ref, send_ref = refs
    received_refs = list(enumerate(reversed(received_refs) if backward else received_refs))
    rows = tokens_ref[...].astype(F32)
    for number, received_ref in received_refs:
        here = (flag_ref[0:1, 0:1] == float(number)) & (flag_ref[1:2, 0:1] == 0.0)
        rows = jnp.where(here, received_ref[...].astype(F32), rows)
    rows = rows.astype(BF)
    rows_ref[...] = rows
    for chip in range(send_ref.shape[0]):
        send_ref[chip] = rows


def row_parts(keep_ref, other_ref):
    first = lax.axis_index("core") == 0
    keep, other = keep_ref[...], other_ref[...]
    return jnp.where(first, keep, other), jnp.where(first, other, keep)


def token_errors(pick_ref, keep_ref, other_ref, targets_ref, send_ref):
    parts = row_parts(keep_ref, other_ref)
    rows = dot(parts[0], pick_ref[0], ((0,), (0,))) + dot(parts[1], pick_ref[1], ((0,), (0,)))
    diff = rows - targets_ref[...].astype(F32)
    total = jnp.sum(diff * diff, 0, keepdims=True)
    last = lax.axis_index("section") == lax.axis_size("section") - 1
    total = jnp.where(last, total, 0.0)
    for number in range(send_ref.shape[0]):
        send_ref[number] = total


def add_up(pieces_ref, send_ref):
    total = pieces_ref[0]
    for number in range(1, pieces_ref.shape[0]):
        total += pieces_ref[number]
    for number in range(send_ref.shape[0]):
        send_ref[number] = total


def finish_losses(pieces_ref, doc_ref, loss_ref):
    total = pieces_ref[0]
    for number in range(1, pieces_ref.shape[0]):
        total += pieces_ref[number]
    count = doc_ref.shape[1]
    mine = doc_ref[...] == iota((DOCS, count), 0)
    sums = jnp.sum(jnp.where(mine, total, 0.0), -1, keepdims=True)
    tokens = jnp.sum(jnp.where(mine, 1.0, 0.0), -1, keepdims=True)
    loss_ref[...] = jnp.broadcast_to(sums / (tokens * D), (DOCS, count))


def place_back(pick_ref, keep_ref, other_ref, out_ref):
    parts = row_parts(keep_ref, other_ref)
    out_ref[...] = (
        dot(pick_ref[0], parts[0], ((0,), (0,))) + dot(pick_ref[1], parts[1], ((0,), (0,)))
    ).astype(BF)


VMEM = pl.BlockSpec(memory_space=pltpu.VMEM)


def run(kernel, outs, *args, flops=0, bytes_accessed=1 << 16):
    several = isinstance(outs, list)
    shapes = [jax.ShapeDtypeStruct(shape, kind) for shape, kind in (outs if several else [outs])]
    return pl.pallas_call(
        kernel,
        out_shape=shapes if several else shapes[0],
        in_specs=[VMEM] * len(args),
        out_specs=[VMEM] * len(shapes) if several else VMEM,
        compiler_params=pltpu.CompilerParams(vmem_limit_bytes=24 * 1024 * 1024),
        cost_estimate=pl.CostEstimate(flops=flops, bytes_accessed=bytes_accessed, transcendentals=0),
    )(*args)


def local(tokens, targets, doc_ids, norm_gains, w_qk, w_val, w_out):
    sections = lax.axis_size("section")
    chips = lax.axis_size("y") * lax.axis_size("x")
    row_count, cols_own = tokens.shape
    cols = 2 * cols_own
    width = 2 * w_qk.shape[2]
    slices = 2
    length = (row_count // 2 + MOST // 2) // slices
    part = slices * length

    def swap(value):
        return lax.ppermute(value, "core", [(0, 1), (1, 0)])

    docs = doc_ids.reshape(1, row_count)
    tokens_t = jnp.swapaxes(tokens, 0, 1)
    picks, bias, first_parts, flags = run(
        prepare,
        [
            ((2, part, row_count), BF),
            ((slices, length, part), F32),
            ((slices, length, cols), BF),
            ((8, 128), F32),
        ],
        docs,
        tokens_t,
        swap(tokens_t),
    )

    first_flags = flags
    keys = jnp.zeros((length, width), F32)
    vals = jnp.zeros((length, width), F32)
    done = jnp.zeros((slices, length, cols), BF)
    received = []
    w_last = w_in = None
    for step in range(sections + slices - 1):
        backward = step % 2 == 1
        rows, send = run(
            functools.partial(spread, backward),
            [((length, cols), BF), ((chips, length, cols), BF)],
            flags,
            first_parts[min(step, slices - 1)],
            *(reversed(received) if backward else received),
        )
        if step == 0:
            w_qk, w_val, w_out, send = lax.optimization_barrier((w_qk, w_val, w_out, send))
            w_out = jnp.swapaxes(w_out[0], 0, 1)
            weights = [w_qk[0], swap(w_qk[0]), w_val[0], swap(w_val[0]), w_out, swap(w_out)]
        gathered = lax.all_to_all(send, PLANE, 0, 0, tiled=True)
        if step == 0:
            w_in, w_last = pl.pallas_call(
                stage,
                out_shape=[
                    jax.ShapeDtypeStruct((D, 2 * width), BF),
                    jax.ShapeDtypeStruct((chips * width, cols), BF),
                ],
                in_specs=[pl.BlockSpec(memory_space=pltpu.HBM)] * 6,
                out_specs=[pl.BlockSpec(memory_space=pltpu.HBM)] * 2,
                scratch_shapes=[
                    pltpu.VMEM(w_out.shape, BF),
                    pltpu.VMEM(w_out.shape, BF),
                    pltpu.VMEM((D, 2 * width), BF),
                    pltpu.VMEM((chips * width, cols), BF),
                    pltpu.SemaphoreType.DMA((8,)),
                ],
                compiler_params=pltpu.CompilerParams(vmem_limit_bytes=60 * 1024 * 1024),
                cost_estimate=pl.CostEstimate(flops=0, bytes_accessed=12 * D * width, transcendentals=0),
            )(*weights)
            gathered, first_parts, w_in, w_last = lax.optimization_barrier((gathered, first_parts, w_in, w_last))
        last = step == sections + slices - 2
        send, *carried = run(
            qkv_attention,
            [((chips, length, width), BF)]
            + ([] if last else [((length, width), F32), ((length, width), F32), ((8, 128), F32)]),
            flags,
            gathered,
            norm_gains,
            w_in,
            bias,
            keys,
            vals,
            flops=4 * length * D * width,
            bytes_accessed=4 * D * width,
        )
        attended = lax.all_to_all(send, PLANE, 0, 0, tiled=True)
        if last:
            attended, picks, targets = lax.optimization_barrier((attended, picks, targets))
        done, *rows = run(
            project_out,
            [((slices, length, cols), BF)] + ([] if last else [((length, cols), BF)]),
            flags,
            attended,
            w_last,
            rows,
            done,
            flops=2 * length * chips * width * cols,
            bytes_accessed=2 * chips * width * cols,
        )
        if last:
            break
        rows = rows[0]
        keys, vals, flags = carried
        received = {}
        for number in reversed(range(slices)):
            z = step - number
            if 0 <= z < sections - 1:
                received[number] = lax.ppermute(rows, "section", [(z, z + 1)])
            else:
                received[number] = jnp.zeros_like(rows)
        received = [received[number] for number in range(slices)]

    part_rows = done.reshape(part, cols)
    halves = [part_rows[:, :cols_own], part_rows[:, cols_own:]]
    own_first = first_flags[2:3, 0:1] == 0.0
    keep = jnp.where(own_first, halves[0], halves[1])
    other = swap(jnp.where(own_first, halves[1], halves[0]))
    targets_t = jnp.swapaxes(targets, 0, 1)
    send = run(token_errors, ((2 * chips, 1, row_count), F32), picks, keep, other, targets_t)
    send = lax.all_to_all(send, PLANE + ("core",), 0, 0, tiled=True)
    send = run(add_up, ((sections, 1, row_count), F32), send)
    send = lax.all_to_all(send, "section", 0, 0, tiled=True)
    losses = run(finish_losses, ((DOCS, row_count), F32), send, docs)[:, 0]

    section_rows = run(place_back, ((row_count, cols_own), BF), picks, keep, other)
    return (section_rows[None], losses)


def solution(mesh):
    names = ("section", "y", "x", "core")
    fine = Mesh(mesh.devices.reshape(mesh.devices.shape[0], 4, 4, 2), names)
    tensor = ("y", "x", "core")
    placed = (
        P(None, tensor),
        P(None, tensor),
        P(),
        P("section", None),
        P("section", None, tensor),
        P("section", None, tensor),
        P("section", None, tensor),
    )
    return jax.shard_map(
        local,
        mesh=fine,
        in_specs=placed,
        out_specs=(P("section", None, tensor), P()),
        check_vma=False,
    )
```

```python
import functools

import jax
import jax.numpy as jnp
from jax import lax
from jax.experimental import pallas as pl
from jax.experimental.pallas import tpu as pltpu
from jax.sharding import Mesh
from jax.sharding import PartitionSpec as P

D = 6144
HD = 64
DOCS = 8
MOST = 32
NEG = -1e30
PLANE = ("y", "x")
BF = jnp.bfloat16
F32 = jnp.float32


def iota(shape, axis):
    return lax.broadcasted_iota(jnp.int32, shape, axis)


def in_core_order(own, other):
    first = lax.axis_index("core") == 0
    return jnp.concatenate([jnp.where(first, own, other), jnp.where(first, other, own)], -1)


def dot(a, b, contract=((1,), (0,))):
    return lax.dot_general(a, b, (contract, ((), ())), preferred_element_type=F32)


def prepare(doc_ref, own_ref, other_ref, pick_ref, bias_ref, rows_ref, flag_ref):
    _, part, count = pick_ref.shape
    length = rows_ref.shape[1]
    doc_j = jnp.broadcast_to(doc_ref[...].astype(F32), (count, count))
    same = jnp.where(doc_j == jnp.transpose(doc_j), 1.0, 0.0)
    before = jnp.where(iota((count, count), 0) < iota((count, count), 1), same, 0.0)
    starts = jnp.sum(before, 0, keepdims=True) == 0.0
    lane = iota((1, count), 1)
    far = (jnp.abs(lane - count // 2) * count + lane).astype(F32)
    nearest = jnp.min(jnp.where(starts, far, float(count * count)), -1, keepdims=True)
    cut = nearest - count * jnp.floor(nearest / count)
    token = iota((part, count), 1).astype(F32)
    slot = iota((part, count), 0).astype(F32)
    picks = [
        jnp.where((token == slot) & (slot < cut), 1.0, 0.0),
        jnp.where(token == slot + cut, 1.0, 0.0),
    ]
    for core in range(2):
        pick_ref[core] = picks[core].astype(BF)
    pick = jnp.where(lax.axis_index("core") == 0, picks[0], picks[1])
    pick_bf = pick.astype(BF)
    rows = in_core_order(*[dot(pick_bf, ref[...], ((1,), (1,))) for ref in (own_ref, other_ref)])
    for number in range(part // length):
        rows_ref[number] = rows[number * length : (number + 1) * length].astype(BF)
    shifted = jnp.concatenate([jnp.zeros((length, count), F32), pick[: part - length]], 0)
    same_bf = same.astype(BF)
    for number, (queries, keys) in enumerate(((pick[:length], shifted), (pick[length:], pick))):
        alike = dot(dot(queries.astype(BF), same_bf).astype(BF), keys.astype(BF), ((1,), (1,)))
        query_at = iota((length, part), 0) + length
        key_at = iota((length, part), 1)
        allowed = ((alike > 0.5) & (key_at <= query_at)) | (key_at == query_at)
        bias_ref[number] = jnp.where(allowed, 0.0, NEG)
    section = lax.axis_index("section")
    row = iota(flag_ref.shape, 0)
    order = jnp.where(row == 0, -section, 0)
    flag_ref[...] = jnp.where((row == 1) & (section == 0), 1, order).astype(F32)


def qkv_attention(
    flag_ref,
    rows_ref,
    gain_ref,
    w_ref,
    bias_ref,
    kin_ref,
    vin_ref,
    send_ref,
    kout_ref=None,
    vout_ref=None,
    next_ref=None,
):
    chips, length, cols = rows_ref.shape
    width = kin_ref.shape[1]
    heads = width // HD
    total = jnp.zeros((length, cols), F32)
    for chip in range(chips):
        total += rows_ref[chip].astype(F32)
    mean = jnp.sum(total, -1, keepdims=True) / (chips * cols)
    total = jnp.zeros((length, cols), F32)
    for chip in range(chips):
        centered = rows_ref[chip].astype(F32) - mean
        total += centered * centered
    scale = lax.rsqrt(jnp.sum(total, -1, keepdims=True) / (chips * cols) + 1e-05)
    acc = jnp.zeros((length, 2 * width), F32)
    for pair in range(0, chips, 2):
        normed = []
        for chip in (pair, pair + 1):
            centered = rows_ref[chip].astype(F32) - mean
            normed.append((centered * scale * gain_ref[:, chip * cols : (chip + 1) * cols]).astype(BF))
        acc += dot(jnp.concatenate(normed, 1), w_ref[pair * cols : (pair + 2) * cols, :])
    rounded = acc.astype(BF).astype(F32)
    qk, val = rounded[:, :width], rounded[:, width:]
    head_of = iota((length, width), 1) // HD
    squares = qk * qk
    inverse = jnp.zeros((length, width), F32)
    stack = []
    for head in range(heads):
        mine = head_of == head
        square_mean = jnp.sum(jnp.where(mine, squares, 0.0), -1, keepdims=True) / HD
        inverse = jnp.where(mine, lax.rsqrt(square_mean + 1e-06), inverse)
        stack.append(jnp.where(mine, qk, 0.0))
    key = (qk * inverse).astype(BF).astype(F32)
    queries = jnp.concatenate(stack, 0).astype(BF)
    keys = jnp.concatenate([kin_ref[...], key], 0).astype(BF)
    vals = jnp.concatenate([vin_ref[...], val], 0).astype(BF)
    bias = jnp.where(flag_ref[0:1, 0:1] > 0.0, bias_ref[1], bias_ref[0])
    scores = dot(queries, keys, ((1,), (1,))) / HD + jnp.concatenate([bias] * heads, 0)
    peak = jnp.max(scores, -1, keepdims=True)
    expo = jnp.exp(scores - peak)
    weights = (expo / jnp.sum(expo, -1, keepdims=True)).astype(BF)
    mixed = dot(weights, vals)
    attended = jnp.zeros((length, width), F32)
    for head in range(heads):
        attended = jnp.where(head_of == head, mixed[head * length : (head + 1) * length], attended)
    half = width // 2
    attended = in_core_order(attended[:, :half], attended[:, half:]).astype(BF)
    for chip in range(chips):
        send_ref[chip] = attended
    if kout_ref is None:
        return
    kout_ref[...] = key
    vout_ref[...] = val
    next_ref[...] = flag_ref[...] + jnp.where(iota(flag_ref.shape, 0) == 0, 1.0, 0.0)


def stage(qk_ref, qk_other_ref, val_ref, val_other_ref, out_ref, out_other_ref, in_ref, last_ref, *scratch):
    own, other, packed, turned, sems = scratch
    width = qk_ref.shape[1]
    copies = [(out_ref, own), (out_other_ref, other)]
    for number, ref in enumerate((qk_ref, qk_other_ref, val_ref, val_other_ref)):
        copies.append((ref, packed.at[:, pl.ds(number * width, width)]))
    copies += [(packed, in_ref), (turned, last_ref)]
    copies = [pltpu.make_async_copy(*pair, sems.at[number]) for number, pair in enumerate(copies)]
    for copy in copies[:6]:
        copy.start()
    for copy in copies[:6]:
        copy.wait()
    copies[6].start()
    block = 256
    first = lax.axis_index("core") == 0
    for begin in range(0, own.shape[1], block):
        span = slice(begin, begin + block)
        here, there = own[:, span], other[:, span]
        here, there = jnp.where(first, here, there), jnp.where(first, there, here)
        turned[span, :] = jnp.transpose(jnp.concatenate([here, there], 0))
    copies[7].start()
    copies[6].wait()
    copies[7].wait()


def project_out(flag_ref, heads_ref, w_ref, rows_ref, kept_ref, done_ref, out_ref=None):
    chips, _, width = heads_ref.shape
    mixed = jnp.zeros(rows_ref.shape, F32)
    for chip in range(chips):
        mixed += dot(heads_ref[chip], w_ref[chip * width : (chip + 1) * width, :])
    rows = (rows_ref[...].astype(F32) + mixed).astype(BF)
    if out_ref is not None:
        out_ref[...] = rows
    for number in range(kept_ref.shape[0]):
        mine = flag_ref[0:1, 0:1] == float(number)
        done_ref[number] = jnp.where(mine, rows.astype(F32), kept_ref[number].astype(F32)).astype(BF)


def spread(backward, flag_ref, tokens_ref, *refs):
    *received_refs, rows_ref, send_ref = refs
    received_refs = list(enumerate(reversed(received_refs) if backward else received_refs))
    rows = tokens_ref[...].astype(F32)
    for number, received_ref in received_refs:
        here = (flag_ref[0:1, 0:1] == float(number)) & (flag_ref[1:2, 0:1] == 0.0)
        rows = jnp.where(here, received_ref[...].astype(F32), rows)
    rows = rows.astype(BF)
    rows_ref[...] = rows
    for chip in range(send_ref.shape[0]):
        send_ref[chip] = rows


def split_columns(done_ref, keep_ref, give_ref):
    half = keep_ref.shape[2]
    first = lax.axis_index("core") == 0
    for number in range(done_ref.shape[0]):
        rows = done_ref[number].astype(F32)
        low, high = rows[:, :half], rows[:, half:]
        keep_ref[number] = jnp.where(first, low, high).astype(BF)
        give_ref[number] = jnp.where(first, high, low).astype(BF)


def row_parts(keep_ref, other_ref):
    first = lax.axis_index("core") == 0
    keep, other = keep_ref[...], other_ref[...]
    return jnp.where(first, keep, other), jnp.where(first, other, keep)


def token_errors(pick_ref, keep_ref, other_ref, targets_ref, send_ref):
    parts = row_parts(keep_ref, other_ref)
    rows = dot(parts[0], pick_ref[0], ((0,), (0,))) + dot(parts[1], pick_ref[1], ((0,), (0,)))
    diff = rows - targets_ref[...].astype(F32)
    total = jnp.sum(diff * diff, 0, keepdims=True)
    last = lax.axis_index("section") == lax.axis_size("section") - 1
    total = jnp.where(last, total, 0.0)
    for number in range(send_ref.shape[0]):
        send_ref[number] = total


def add_up(pieces_ref, send_ref):
    total = pieces_ref[0]
    for number in range(1, pieces_ref.shape[0]):
        total += pieces_ref[number]
    for number in range(send_ref.shape[0]):
        send_ref[number] = total


def finish_losses(pieces_ref, doc_ref, loss_ref):
    total = pieces_ref[0]
    for number in range(1, pieces_ref.shape[0]):
        total += pieces_ref[number]
    count = doc_ref.shape[1]
    mine = doc_ref[...] == iota((DOCS, count), 0)
    sums = jnp.sum(jnp.where(mine, total, 0.0), -1, keepdims=True)
    tokens = jnp.sum(jnp.where(mine, 1.0, 0.0), -1, keepdims=True)
    loss_ref[...] = jnp.broadcast_to(sums / (tokens * D), (DOCS, count))


def place_back(pick_ref, keep_ref, other_ref, out_ref):
    parts = row_parts(keep_ref, other_ref)
    out_ref[...] = (
        dot(pick_ref[0], parts[0], ((0,), (0,))) + dot(pick_ref[1], parts[1], ((0,), (0,)))
    ).astype(BF)


VMEM = pl.BlockSpec(memory_space=pltpu.VMEM)


def run(kernel, outs, *args, flops=0, bytes_accessed=1 << 16):
    several = isinstance(outs, list)
    shapes = [jax.ShapeDtypeStruct(shape, kind) for shape, kind in (outs if several else [outs])]
    return pl.pallas_call(
        kernel,
        out_shape=shapes if several else shapes[0],
        in_specs=[VMEM] * len(args),
        out_specs=[VMEM] * len(shapes) if several else VMEM,
        compiler_params=pltpu.CompilerParams(vmem_limit_bytes=24 * 1024 * 1024),
        cost_estimate=pl.CostEstimate(flops=flops, bytes_accessed=bytes_accessed, transcendentals=0),
    )(*args)


def local(tokens, targets, doc_ids, norm_gains, w_qk, w_val, w_out):
    sections = lax.axis_size("section")
    chips = lax.axis_size("y") * lax.axis_size("x")
    row_count, cols_own = tokens.shape
    cols = 2 * cols_own
    width = 2 * w_qk.shape[2]
    slices = 2
    length = (row_count // 2 + MOST // 2) // slices
    part = slices * length

    def swap(value):
        return lax.ppermute(value, "core", [(0, 1), (1, 0)])

    docs = doc_ids.reshape(1, row_count)
    tokens_t = jnp.swapaxes(tokens, 0, 1)
    picks, bias, first_parts, flags = run(
        prepare,
        [
            ((2, part, row_count), BF),
            ((slices, length, part), F32),
            ((slices, length, cols), BF),
            ((8, 128), F32),
        ],
        docs,
        tokens_t,
        swap(tokens_t),
    )

    keys = jnp.zeros((length, width), F32)
    vals = jnp.zeros((length, width), F32)
    done = jnp.zeros((slices, length, cols), BF)
    received = []
    w_last = w_in = None
    for step in range(sections + slices - 1):
        backward = step % 2 == 1
        rows, send = run(
            functools.partial(spread, backward),
            [((length, cols), BF), ((chips, length, cols), BF)],
            flags,
            first_parts[min(step, slices - 1)],
            *(reversed(received) if backward else received),
        )
        if step == 0:
            w_qk, w_val, w_out, send = lax.optimization_barrier((w_qk, w_val, w_out, send))
            w_out = jnp.swapaxes(w_out[0], 0, 1)
            weights = [w_qk[0], swap(w_qk[0]), w_val[0], swap(w_val[0]), w_out, swap(w_out)]
        gathered = lax.all_to_all(send, PLANE, 0, 0, tiled=True)
        if step == 0:
            w_in, w_last = pl.pallas_call(
                stage,
                out_shape=[
                    jax.ShapeDtypeStruct((D, 2 * width), BF),
                    jax.ShapeDtypeStruct((chips * width, cols), BF),
                ],
                in_specs=[pl.BlockSpec(memory_space=pltpu.HBM)] * 6,
                out_specs=[pl.BlockSpec(memory_space=pltpu.HBM)] * 2,
                scratch_shapes=[
                    pltpu.VMEM(w_out.shape, BF),
                    pltpu.VMEM(w_out.shape, BF),
                    pltpu.VMEM((D, 2 * width), BF),
                    pltpu.VMEM((chips * width, cols), BF),
                    pltpu.SemaphoreType.DMA((8,)),
                ],
                compiler_params=pltpu.CompilerParams(vmem_limit_bytes=60 * 1024 * 1024),
                cost_estimate=pl.CostEstimate(flops=0, bytes_accessed=12 * D * width, transcendentals=0),
            )(*weights)
            gathered, first_parts, w_in, w_last = lax.optimization_barrier((gathered, first_parts, w_in, w_last))
        last = step == sections + slices - 2
        send, *carried = run(
            qkv_attention,
            [((chips, length, width), BF)]
            + ([] if last else [((length, width), F32), ((length, width), F32), ((8, 128), F32)]),
            flags,
            gathered,
            norm_gains,
            w_in,
            bias,
            keys,
            vals,
            flops=4 * length * D * width,
            bytes_accessed=4 * D * width,
        )
        attended = lax.all_to_all(send, PLANE, 0, 0, tiled=True)
        if last:
            attended, picks, targets = lax.optimization_barrier((attended, picks, targets))
        done, *rows = run(
            project_out,
            [((slices, length, cols), BF)] + ([] if last else [((length, cols), BF)]),
            flags,
            attended,
            w_last,
            rows,
            done,
            flops=2 * length * chips * width * cols,
            bytes_accessed=2 * chips * width * cols,
        )
        if last:
            break
        rows = rows[0]
        keys, vals, flags = carried
        received = {}
        for number in reversed(range(slices)):
            z = step - number
            if 0 <= z < sections - 1:
                received[number] = lax.ppermute(rows, "section", [(z, z + 1)])
            else:
                received[number] = jnp.zeros_like(rows)
        received = [received[number] for number in range(slices)]

    keep, give = run(split_columns, [((slices, length, cols_own), BF)] * 2, done)
    keep = keep.reshape(part, cols_own)
    other = swap(give.reshape(part, cols_own))
    targets_t = jnp.swapaxes(targets, 0, 1)
    send = run(token_errors, ((2 * chips, 1, row_count), F32), picks, keep, other, targets_t)
    send = lax.all_to_all(send, PLANE + ("core",), 0, 0, tiled=True)
    send = run(add_up, ((sections, 1, row_count), F32), send)
    send = lax.all_to_all(send, "section", 0, 0, tiled=True)
    losses = run(finish_losses, ((DOCS, row_count), F32), send, docs)[:, 0]

    section_rows = run(place_back, ((row_count, cols_own), BF), picks, keep, other)
    return (section_rows[None], losses)


def solution(mesh):
    names = ("section", "y", "x", "core")
    fine = Mesh(mesh.devices.reshape(mesh.devices.shape[0], 4, 4, 2), names)
    tensor = ("y", "x", "core")
    placed = (
        P(None, tensor),
        P(None, tensor),
        P(),
        P("section", None),
        P("section", None, tensor),
        P("section", None, tensor),
        P("section", None, tensor),
    )
    return jax.shard_map(
        local,
        mesh=fine,
        in_specs=placed,
        out_specs=(P("section", None, tensor), P()),
        check_vma=False,
    )
```
